32 devices in a mesh: section: 4 (over y, x), seqtp: 8 (over z, core).
Axes of the slice: x: 2, y: 2, z: 4, core: 2. Of those that a mesh axis runs over, the one named last changes fastest.
Arguments:
- saved_in: bfloat16 [4, 4, 16, 4096], P('section', None, 'seqtp'), may hold values from -40 to 40
- grad_in: bfloat16 [4, 16, 4096], P('section', 'seqtp'), may hold values from -6 to 6
- slot_table: int32 [4], P('section'), may hold values from 0 to 3
- gain: bfloat16 [4, 4096], P('section'), may hold values from 0.099609375 to 1.8984375
- w_gate: bfloat16 [4096, 3072], P(None, 'seqtp'), may hold values from -0.09375 to 0.09375
- w_up: bfloat16 [4096, 3072], P(None, 'seqtp'), may hold values from -0.09375 to 0.09375
- w_down: bfloat16 [3072, 4096], P('seqtp'), may hold values from -0.109375 to 0.109375
Outputs:
- grad_prev: bfloat16 [4, 16, 4096], P('section', 'seqtp')
The draws below stay inside these ranges and needn't reach their ends.
All inputs are finite; a program needn't handle non-finite values.
Results may differ from the reference program's by a relative error of at most 0.0052.
Values may be sent and summed in bfloat16 or wider, within the bound.
No kernel may reach another device: no remote copies, remote signals or barrier semaphores. Data moves between devices by JAX's collectives and lax.ppermute only.
A program may use at most 64 MiB of HBM per device.

```python
import math
import jax
import jax.numpy as jnp
from jax import lax

D = 4096
FF = 3072
TOKENS = 16
SLOTS = 4
SECTIONS = 4


def scaled_activation(key, shape):
    key_normal, key_rows, key_cols = jax.random.split(key, 3)
    low_end = math.log(0.3)
    high_end = math.log(3.0)
    row_scale = jnp.exp(jax.random.uniform(key_rows, shape[:-1] + (1,), jnp.float32, low_end, high_end))
    col_scale = jnp.exp(jax.random.uniform(key_cols, (shape[-1],), jnp.float32, low_end, high_end))
    base_values = jax.random.normal(key_normal, shape, jnp.float32)
    return jnp.clip(base_values * row_scale * col_scale, -40.0, 40.0)


def draw_saved_in(key, part):
    return scaled_activation(jax.random.fold_in(key, 23), (SECTIONS, SLOTS, TOKENS, D)).astype(jnp.bfloat16)


def draw_slot_table(key, part):
    key_values, key_place = jax.random.split(jax.random.fold_in(key, 37))
    values = jax.random.randint(key_values, (SECTIONS,), 0, SLOTS, jnp.int32)
    where_top = jax.random.randint(key_place, (), 0, SECTIONS, jnp.int32)
    values = values.at[where_top].set(SLOTS - 1)
    values = values.at[(where_top + 1) % SECTIONS].set(0)
    return values.astype(jnp.int32)


def steps_of(key, shape, cuts, low, high):
    loudness = 1.0
    for dim, parts in cuts:
        heights = jax.random.uniform(jax.random.fold_in(jax.random.fold_in(key, 6), dim), (parts,), jnp.float32, low / len(cuts), high / len(cuts))
        loudness = loudness * jnp.repeat(jnp.exp(heights), shape[dim] // parts).reshape((-1,) + (1,) * (len(shape) - 1 - dim))
    return loudness


def noise(key, extent, scale, reach, shards=(), dtype=jnp.bfloat16):
    values = scale * jax.random.normal(key, extent, jnp.float32)
    if shards:
        values = values * steps_of(key, extent, shards, -0.22, 0.18)
    return jnp.clip(values, -reach, reach).astype(dtype)


def setup_inputs(seed: int = 0) -> dict:
    splits = jax.random.split(jax.random.key(seed), 8)
    return {
        "saved_in": draw_saved_in(jax.random.fold_in(splits[7], 71), 0),
        "grad_in": noise(splits[1], (SECTIONS, TOKENS, D), 1.0, 6.0, ((0, 4), (1, 8))),
        "slot_table": draw_slot_table(jax.random.fold_in(splits[7], 71), 0),
        "gain": jnp.clip(1.0 + 0.18 * jax.random.normal(splits[3], (SECTIONS, D), jnp.float32), 0.099609375, 1.8984375).astype(jnp.bfloat16),
        "w_gate": noise(splits[4], (D, FF), D ** -0.5, 0.09375, ((1, 8),)),
        "w_up": noise(splits[5], (D, FF), D ** -0.5, 0.09375, ((1, 8),)),
        "w_down": noise(splits[6], (FF, D), FF ** -0.5, 0.109375, ((0, 8),)),
    }


EPS = 1e-05

def rms_norm(values, gain_vec):
    wide = values.astype(jnp.float32)
    recip = lax.rsqrt(lax.optimization_barrier(jnp.mean(wide * wide, axis=-1, keepdims=True)) + EPS)
    return ((wide * recip * gain_vec).astype(jnp.bfloat16), recip)

def transposed(left, weight):
    return lax.dot_general(left, weight, (((1,), (1,)), ((), ())), preferred_element_type=jnp.float32)

def reference(saved_in, grad_in, slot_table, gain, w_gate, w_up, w_down):

    def one_section(operands):
        saved, cotangent, slot, gain_row = operands
        gain_vec = gain_row.astype(jnp.float32)
        behind = lax.dynamic_index_in_dim(saved, slot.astype(jnp.int32), 0, keepdims=False)
        normed_b, recip_b = rms_norm(behind, gain_vec)
        gate_b = jnp.dot(normed_b, w_gate, preferred_element_type=jnp.float32)
        up_b = jnp.dot(normed_b, w_up, preferred_element_type=jnp.float32)
        d_hidden = transposed(cotangent, w_down)
        probe = jax.nn.sigmoid(gate_b)
        d_gate = (d_hidden * up_b * probe * (1.0 + gate_b * (1.0 - probe))).astype(jnp.bfloat16)
        d_up = (d_hidden * gate_b * probe).astype(jnp.bfloat16)
        d_normed = transposed(d_gate, w_gate) + transposed(d_up, w_up)
        scaled = gain_vec * d_normed
        unit = behind.astype(jnp.float32) * recip_b
        grad_x = cotangent.astype(jnp.float32) + recip_b * (scaled - unit * lax.optimization_barrier(jnp.mean(scaled * unit, axis=-1, keepdims=True)))
        return grad_x.astype(jnp.bfloat16)
    grads = lax.map(one_section, (saved_in, grad_in, slot_table, gain))
    return jnp.roll(grads, -1, axis=0)
```

```python
import functools

import jax
import jax.numpy as jnp
from jax import lax
from jax.experimental import pallas as pl
from jax.experimental.pallas import tpu as pltpu
from jax.sharding import PartitionSpec as P

EPS = 1e-05
CORES = 2


def whole(n):
    return [pl.BlockSpec(memory_space=pltpu.VMEM)] * n


def params(mib):
    return pltpu.CompilerParams(vmem_limit_bytes=mib * 2**20)


def prepare(slot_ref, saved_ref, grad_ref, gain_ref, sent_ref, own_ref):
    d = grad_ref.shape[-1]
    behind = saved_ref[0, slot_ref[0]]
    wide = behind.astype(jnp.float32)
    gain = gain_ref[...].astype(jnp.float32)
    recip = lax.rsqrt(jnp.mean(wide * wide, axis=-1, keepdims=True) + EPS)
    grad = grad_ref[0]
    sent_ref[:, :d] = (wide * recip * gain).astype(jnp.bfloat16)
    sent_ref[:, d:] = grad
    own_ref[:, :d] = behind
    own_ref[:, d : 2 * d] = grad
    half = d // 2
    own_ref[0:1, 2 * d :] = gain_ref[:, :half]
    own_ref[1:2, 2 * d :] = gain_ref[:, half:]


def nt(left, weight):
    return lax.dot_general(
        left, weight, (((1,), (1,)), ((), ())), preferred_element_type=jnp.float32
    )


def expert(n_near, *refs):
    near, (far_ref, gate_ref, up_ref, down_ref, mine_ref, other_ref, rows_ref) = (
        refs[:n_near],
        refs[n_near:],
    )
    d = gate_ref.shape[0]
    r = near[0].shape[0]
    for k, ref in enumerate(near):
        rows_ref[k * r : (k + 1) * r] = ref[...].astype(jnp.float32)
        rows_ref[(n_near + k) * r : (n_near + k + 1) * r] = far_ref[k].astype(jnp.float32)
    normed = rows_ref[:, :d].astype(jnp.bfloat16)
    grad = rows_ref[:, d:].astype(jnp.bfloat16)
    gate = jnp.dot(normed, gate_ref[...], preferred_element_type=jnp.float32)
    up = jnp.dot(normed, up_ref[...], preferred_element_type=jnp.float32)
    d_hidden = nt(grad, down_ref[...])
    p = jax.nn.sigmoid(gate)
    d_gate = (d_hidden * up * p * (1.0 + gate * (1.0 - p))).astype(jnp.bfloat16)
    d_up = (d_hidden * gate * p).astype(jnp.bfloat16)
    total = nt(d_gate, gate_ref[...]) + nt(d_up, up_ref[...])
    half = n_near * r
    mine_ref[...] = total[:half]
    other_ref[...] = total[half:]


def add_cores(n_near, mine_ref, got_ref, *out_refs):
    r = out_refs[0].shape[0]
    total = mine_ref[...] + got_ref[...]
    for k, ref in enumerate(out_refs):
        ref[...] = total[k * r : (k + 1) * r].astype(ref.dtype)


def finish(n_near, own_ref, *refs):
    parts, out_ref, gain_ref = refs[:n_near], refs[n_near], refs[n_near + 1]
    d = parts[0].shape[-1]
    half = d // 2
    gain_ref[:, :half] = own_ref[0:1, 2 * d :].astype(jnp.float32)
    gain_ref[:, half:] = own_ref[1:2, 2 * d :].astype(jnp.float32)
    total = sum(ref[...].astype(jnp.float32) for ref in parts)
    wide = own_ref[:, :d].astype(jnp.float32)
    grad = own_ref[:, d : 2 * d].astype(jnp.float32)
    recip = lax.rsqrt(jnp.mean(wide * wide, axis=-1, keepdims=True) + EPS)
    scaled = gain_ref[...] * total
    unit = wide * recip
    mean = jnp.mean(scaled * unit, axis=-1, keepdims=True)
    out_ref[0] = (grad + recip * (scaled - unit * mean)).astype(out_ref.dtype)


def on_device(sections, members, saved_in, grad_in, slot_table, gain, w_gate, w_up, w_down):
    chips = members // CORES
    r, d = grad_in.shape[1:]
    f32, bf16 = jnp.float32, jnp.bfloat16
    shape = jax.ShapeDtypeStruct
    far_first = [k for k in range(chips - 1, 0, -1)]

    def near(i, k):
        chip, core = divmod(i, CORES)
        return (chip ^ k if chips & (chips - 1) == 0 else (chip + k) % chips) * CORES + core

    def to_chip(x, k):
        return lax.ppermute(x, "seqtp", [(i, near(i, k)) for i in range(members)])

    def to_core(x):
        return lax.ppermute(x, "seqtp", [(i, i ^ 1) for i in range(members)])

    def home(x, k):
        pairs = [
            (s * members + near(i, k), (s - 1) % sections * members + i)
            for s in range(sections)
            for i in range(members)
        ]
        return lax.ppermute(x, ("section", "seqtp"), pairs)

    sent, own = pl.pallas_call(
        prepare,
        out_shape=[shape((r, 2 * d), bf16), shape((r, 2 * d + d // 2), bf16)],
        in_specs=[pl.BlockSpec(memory_space=pltpu.SMEM)] + whole(3),
        out_specs=whole(2),
        name="prepare",
    )(slot_table, saved_in, grad_in, gain)
    blocks = {0: sent}
    for k in far_first:
        blocks[k] = to_chip(sent, k)
    blocks = [blocks[k] for k in range(chips)]
    far = to_core(jnp.stack(blocks))
    mine, other = pl.pallas_call(
        functools.partial(expert, chips),
        out_shape=[shape((chips * r, d), f32)] * 2,
        in_specs=whole(chips + 4),
        out_specs=whole(2),
        scratch_shapes=[pltpu.VMEM((members * r, 2 * d), f32)],
        compiler_params=params(24),
        name="expert",
    )(*blocks, far, w_gate, w_up, w_down)
    got = to_core(other)
    sums = pl.pallas_call(
        functools.partial(add_cores, chips),
        out_shape=[shape((r, d), bf16)] * chips,
        in_specs=whole(2),
        out_specs=whole(chips),
        name="add_cores",
    )(mine, got)
    landed = {}
    for k in far_first + [0]:
        landed[k] = home(sums[k], k)
    own = home(own, 0)
    return pl.pallas_call(
        functools.partial(finish, chips),
        out_shape=shape((1, r, d), bf16),
        in_specs=whole(chips + 1),
        out_specs=pl.BlockSpec(memory_space=pltpu.VMEM),
        scratch_shapes=[pltpu.VMEM((1, d), f32)],
        name="finish",
    )(own, *[landed[k] for k in range(chips)])


def solution(mesh):
    return jax.shard_map(
        functools.partial(on_device, mesh.shape["section"], mesh.shape["seqtp"]),
        mesh=mesh,
        in_specs=(
            P("section", None, "seqtp", None),
            P("section", "seqtp", None),
            P("section"),
            P("section", None),
            P(None, "seqtp"),
            P(None, "seqtp"),
            P("seqtp", None),
        ),
        out_specs=P("section", "seqtp", None),
        check_vma=False,
    )
```

```python
import functools

import jax
import jax.numpy as jnp
from jax import lax
from jax.experimental import pallas as pl
from jax.experimental.pallas import tpu as pltpu
from jax.sharding import PartitionSpec as P

EPS = 1e-05
CORES = 2


VMEM = pltpu.VMEM


def whole(n):
    return [pl.BlockSpec(memory_space=VMEM)] * n


def near_core(*arrays):
    return [pltpu.with_memory_space_constraint(x, VMEM) for x in arrays]


def params(mib):
    return pltpu.CompilerParams(vmem_limit_bytes=mib * 2**20)


def prepare(slot_hbm, saved_hbm, grad_hbm, gain_hbm, sent_ref, own_ref, *scratch):
    slot_ref, saved_ref, grad_ref, gain_ref, sems = scratch
    copies = [
        pltpu.make_async_copy(src, dst, sems.at[i])
        for i, (src, dst) in enumerate(
            zip((slot_hbm, saved_hbm, grad_hbm, gain_hbm), scratch)
        )
    ]
    for copy in copies:
        copy.start()
    for copy in copies:
        copy.wait()
    d = grad_ref.shape[-1]
    behind = saved_ref[0, slot_ref[0]]
    wide = behind.astype(jnp.float32)
    gain = gain_ref[...].astype(jnp.float32)
    recip = lax.rsqrt(jnp.mean(wide * wide, axis=-1, keepdims=True) + EPS)
    grad = grad_ref[0]
    sent_ref[:, :d] = (wide * recip * gain).astype(jnp.bfloat16)
    sent_ref[:, d:] = grad
    own_ref[:, :d] = behind
    own_ref[:, d : 2 * d] = grad
    half = d // 2
    own_ref[0:1, 2 * d :] = gain_ref[:, :half]
    own_ref[1:2, 2 * d :] = gain_ref[:, half:]


def stack(n, *refs):
    out_ref = refs[-1]
    r = refs[0].shape[0]
    for k, ref in enumerate(refs[:n]):
        out_ref[k * r : (k + 1) * r] = ref[...]


def nt(left, weight):
    return lax.dot_general(
        left, weight, (((1,), (1,)), ((), ())), preferred_element_type=jnp.float32
    )


def fetch(gate_hbm, up_hbm, down_hbm, both_ref, down_ref, sems):
    d, h = gate_hbm.shape
    parts = sems.shape[1]
    copies = []
    for n in range(parts):
        rows, cols = pl.ds(n * d // parts, d // parts), pl.ds(n * h // parts, h // parts)
        copies += [
            pltpu.make_async_copy(gate_hbm.at[rows], both_ref.at[rows, :h], sems.at[0, n]),
            pltpu.make_async_copy(up_hbm.at[rows], both_ref.at[rows, h:], sems.at[1, n]),
            pltpu.make_async_copy(down_hbm.at[cols], down_ref.at[cols], sems.at[2, n]),
        ]
    for copy in copies:
        copy.start()
    for copy in copies:
        copy.wait()


def expert(*refs):
    *blocks, both_ref, down_ref, mine_ref, other_ref, rows_ref = refs
    d, h2 = both_ref.shape
    h = h2 // 2
    r = blocks[0].shape[0]
    for k, ref in enumerate(blocks):
        rows_ref[k * r : (k + 1) * r] = ref[...].astype(jnp.float32)
    normed = rows_ref[:, :d].astype(jnp.bfloat16)
    grad = rows_ref[:, d:].astype(jnp.bfloat16)
    both = jnp.dot(normed, both_ref[...], preferred_element_type=jnp.float32)
    gate, up = both[:, :h], both[:, h:]
    d_hidden = nt(grad, down_ref[...])
    p = jax.nn.sigmoid(gate)
    d_gate = d_hidden * up * p * (1.0 + gate * (1.0 - p))
    d_up = d_hidden * gate * p
    d_both = jnp.concatenate([d_gate, d_up], axis=1).astype(jnp.bfloat16)
    total = nt(d_both, both_ref[...])
    half = total.shape[0] // 2
    mine_ref[...] = total[:half]
    other_ref[...] = total[half:]


def add_cores(mine_ref, got_ref, *out_refs):
    total = mine_ref[...] + got_ref[...]
    r = out_refs[0].shape[0]
    for k, ref in enumerate(out_refs):
        ref[...] = total[k * r : (k + 1) * r].astype(ref.dtype)


def add_chips(*refs):
    *parts, keep_ref, send_ref = refs
    total = sum(ref[...].astype(jnp.float32) for ref in parts)
    r = keep_ref.shape[0]
    keep_ref[...] = total[:r]
    send_ref[...] = total[r:]


def finish(own_ref, keep_ref, got_ref, out_ref, gain_ref):
    d = out_ref.shape[-1]
    half = d // 2
    gain_ref[:, :half] = own_ref[0:1, 2 * d :].astype(jnp.float32)
    gain_ref[:, half:] = own_ref[1:2, 2 * d :].astype(jnp.float32)
    wide = own_ref[:, :d].astype(jnp.float32)
    grad = own_ref[:, d : 2 * d].astype(jnp.float32)
    recip = lax.rsqrt(jnp.mean(wide * wide, axis=-1, keepdims=True) + EPS)
    scaled = gain_ref[...] * (keep_ref[...] + got_ref[...])
    unit = wide * recip
    mean = jnp.mean(scaled * unit, axis=-1, keepdims=True)
    out_ref[0] = (grad + recip * (scaled - unit * mean)).astype(out_ref.dtype)


def on_device(sections, members, saved_in, grad_in, slot_table, gain, w_gate, w_up, w_down):
    chips = members // CORES
    r, d = grad_in.shape[1:]
    f32, bf16 = jnp.float32, jnp.bfloat16
    shape = jax.ShapeDtypeStruct
    served = [list(range(chips - 1 - c, -1, -CORES)) for c in range(CORES)]
    steps = [list(ks) for ks in zip(*served)][::-1]

    def near(i, ks):
        chip, core = divmod(i, CORES)
        k = ks[core]
        return (chip ^ k if chips & (chips - 1) == 0 else (chip + k) % chips) * CORES + core

    def to_chip(x, ks):
        return lax.ppermute(x, "seqtp", [(i, near(i, ks)) for i in range(members)])

    def to_core(x):
        return lax.ppermute(x, "seqtp", [(i, i ^ 1) for i in range(members)])

    def home(x, ks):
        pairs = [
            (s * members + near(i, ks), (s - 1) % sections * members + i)
            for s in range(sections)
            for i in range(members)
        ]
        return lax.ppermute(x, ("section", "seqtp"), pairs)

    sent, own = pl.pallas_call(
        prepare,
        out_shape=[VMEM((r, 2 * d), bf16), VMEM((r, 2 * d + d // 2), bf16)],
        in_specs=[pl.BlockSpec(memory_space=pl.ANY)] * 4,
        out_specs=whole(2),
        scratch_shapes=[
            pltpu.SMEM(slot_table.shape, slot_table.dtype),
            VMEM(saved_in.shape, bf16),
            VMEM(grad_in.shape, bf16),
            VMEM(gain.shape, bf16),
            pltpu.SemaphoreType.DMA((4,)),
        ],
        compiler_params=params(4),
        name="prepare",
    )(*[slot_table] + [pltpu.with_memory_space_constraint(x, pltpu.HBM) for x in (saved_in, grad_in, gain)])
    def stacked(parts, after=()):
        rows = sum(part.shape[0] for part in parts)
        return pl.pallas_call(
            functools.partial(stack, len(parts)),
            out_shape=VMEM((rows,) + parts[0].shape[1:], bf16),
            in_specs=whole(len(parts)) + [pl.BlockSpec(memory_space=pl.ANY)] * len(after),
            out_specs=pl.BlockSpec(memory_space=VMEM),
            compiler_params=params(4),
            name="stack",
        )(*near_core(*parts, *after))

    chip_rows = stacked([sent, to_core(sent)])
    hidden = w_down.shape[0]
    weights = pl.pallas_call(
        fetch,
        out_shape=[VMEM((d, 2 * hidden), bf16), VMEM((hidden, d), bf16)],
        in_specs=[pl.BlockSpec(memory_space=pl.ANY)] * 3,
        out_specs=whole(2),
        scratch_shapes=[pltpu.SemaphoreType.DMA((3, 1))],
        compiler_params=params(4),
        cost_estimate=pl.CostEstimate(flops=0, bytes_accessed=12 * d * hidden, transcendentals=0),
        name="fetch",
    )(*[pltpu.with_memory_space_constraint(x, pltpu.HBM) for x in (w_gate, w_up, w_down)])
    blocks = [to_chip(chip_rows, ks) for ks in steps[::-1]][::-1]
    block = stacked(blocks, weights)
    blocks = [block, to_core(block)]
    rows = block.shape[0]
    mine, other = pl.pallas_call(
        expert,
        out_shape=[VMEM((rows, d), f32)] * 2,
        in_specs=whole(len(blocks) + 2),
        out_specs=whole(2),
        scratch_shapes=[VMEM((2 * rows, 2 * d), f32)],
        compiler_params=params(16),
        name="expert",
    )(*near_core(*blocks, *weights))
    sums = pl.pallas_call(
        add_cores,
        out_shape=[VMEM((CORES * r, d), bf16)] * len(steps),
        in_specs=whole(2),
        out_specs=whole(len(steps)),
        compiler_params=params(4),
        name="add_cores",
    )(*near_core(mine, to_core(other)))
    landed = [home(block, ks) for block, ks in zip(sums[::-1], steps[::-1])]
    own = home(own, [0] * CORES)
    keep, send = pl.pallas_call(
        add_chips,
        out_shape=[VMEM((r, d), f32)] * 2,
        in_specs=whole(len(steps)),
        out_specs=whole(2),
        compiler_params=params(4),
        name="add_chips",
    )(*near_core(*landed))
    return pl.pallas_call(
        finish,
        out_shape=shape((1, r, d), bf16),
        in_specs=whole(3),
        out_specs=pl.BlockSpec(memory_space=VMEM),
        scratch_shapes=[VMEM((1, d), f32)],
        compiler_params=params(4),
        name="finish",
    )(*near_core(own, keep, to_core(send)))


def solution(mesh):
    return jax.shard_map(
        functools.partial(on_device, mesh.shape["section"], mesh.shape["seqtp"]),
        mesh=mesh,
        in_specs=(
            P("section", None, "seqtp", None),
            P("section", "seqtp", None),
            P("section"),
            P("section", None),
            P(None, "seqtp"),
            P(None, "seqtp"),
            P("seqtp", None),
        ),
        out_specs=P("section", "seqtp", None),
        check_vma=False,
    )
```

```python
import functools

import jax
import jax.numpy as jnp
from jax import lax
from jax.experimental import pallas as pl
from jax.experimental.pallas import tpu as pltpu
from jax.sharding import PartitionSpec as P

EPS = 1e-05
CORES = 2


VMEM = pltpu.VMEM


def whole(n):
    return [pl.BlockSpec(memory_space=VMEM)] * n


def near_core(*arrays):
    return [pltpu.with_memory_space_constraint(x, VMEM) for x in arrays]


def params(mib):
    return pltpu.CompilerParams(vmem_limit_bytes=mib * 2**20)


def prepare(slot_hbm, saved_hbm, grad_hbm, gain_hbm, sent_ref, own_ref, *scratch):
    slot_ref, saved_ref, grad_ref, gain_ref, sems = scratch
    copies = [
        pltpu.make_async_copy(src, dst, sems.at[i])
        for i, (src, dst) in enumerate(
            zip((slot_hbm, saved_hbm, grad_hbm, gain_hbm), scratch)
        )
    ]
    for copy in copies:
        copy.start()
    for copy in copies:
        copy.wait()
    d = grad_ref.shape[-1]
    behind = saved_ref[0, slot_ref[0]]
    wide = behind.astype(jnp.float32)
    gain = gain_ref[...].astype(jnp.float32)
    recip = lax.rsqrt(jnp.mean(wide * wide, axis=-1, keepdims=True) + EPS)
    grad = grad_ref[0]
    sent_ref[:, :d] = (wide * recip * gain).astype(jnp.bfloat16)
    sent_ref[:, d:] = grad
    own_ref[:, :d] = behind
    own_ref[:, d : 2 * d] = grad
    half = d // 2
    own_ref[0:1, 2 * d :] = gain_ref[:, :half]
    own_ref[1:2, 2 * d :] = gain_ref[:, half:]


def stack(n, *refs):
    out_ref = refs[-1]
    r = refs[0].shape[0]
    for k, ref in enumerate(refs[:n]):
        out_ref[k * r : (k + 1) * r] = ref[...]


def nn(left, weight):
    return jnp.dot(left, weight, preferred_element_type=jnp.float32)


def nt(left, weight):
    return lax.dot_general(
        left, weight, (((1,), (1,)), ((), ())), preferred_element_type=jnp.float32
    )


def fetch(gate_hbm, up_hbm, both_ref, turned_ref, sems, up_sem):
    d, h = gate_hbm.shape
    parts = sems.shape[0]
    rows = d // parts
    copies = [
        pltpu.make_async_copy(
            gate_hbm.at[pl.ds(n * rows, rows)], both_ref.at[pl.ds(n * rows, rows), pl.ds(0, h)], sems.at[n]
        )
        for n in range(parts)
    ]
    up = pltpu.make_async_copy(up_hbm, both_ref.at[:, pl.ds(h, h)], up_sem)
    for copy in copies + [up]:
        copy.start()
    for n, copy in enumerate(copies):
        copy.wait()
        turned_ref[:, n * rows : (n + 1) * rows] = both_ref[n * rows : (n + 1) * rows, :h].T
    up.wait()


def turn(both_ref, after, turned_ref):
    h, d = turned_ref.shape
    step = d // 8
    for n in range(0, d, step):
        turned_ref[:, n : n + step] = both_ref[n : n + step, h:].T


def arrange(*refs):
    *blocks, normed_ref, grad_ref, rows_ref = refs
    d = normed_ref.shape[1]
    r = blocks[0].shape[0]
    for k, ref in enumerate(blocks):
        rows_ref[k * r : (k + 1) * r] = ref[...].astype(jnp.float32)
    normed_ref[...] = rows_ref[:, :d].astype(jnp.bfloat16)
    grad_ref[...] = rows_ref[:, d:].astype(jnp.bfloat16)


def expert(normed_ref, hidden_ref, both_ref, gate_ref, up_ref, mine_ref, other_ref):
    h = hidden_ref.shape[1]
    gate = nn(normed_ref[...], both_ref[:, :h])
    up = nn(normed_ref[...], both_ref[:, h:])
    d_hidden = hidden_ref[...]
    p = jax.nn.sigmoid(gate)
    d_gate = d_hidden * up * p * (1.0 + gate * (1.0 - p))
    d_up = d_hidden * gate * p
    d_both = jnp.concatenate([d_gate, d_up], axis=1).astype(jnp.bfloat16)
    total = nn(d_both[:, :h], gate_ref[...]) + nn(d_both[:, h:], up_ref[...])
    half = total.shape[0] // 2
    mine_ref[...] = total[:half]
    other_ref[...] = total[half:]


def add_cores(mine_ref, got_ref, *out_refs):
    total = mine_ref[...] + got_ref[...]
    r = out_refs[0].shape[0]
    for k, ref in enumerate(out_refs):
        ref[...] = total[k * r : (k + 1) * r].astype(ref.dtype)


def add_chips(*refs):
    *parts, keep_ref, send_ref = refs
    total = sum(ref[...].astype(jnp.float32) for ref in parts)
    r = keep_ref.shape[0]
    keep_ref[...] = total[:r]
    send_ref[...] = total[r:]


def finish(own_ref, keep_ref, got_ref, out_ref, gain_ref):
    d = out_ref.shape[-1]
    half = d // 2
    gain_ref[:, :half] = own_ref[0:1, 2 * d :].astype(jnp.float32)
    gain_ref[:, half:] = own_ref[1:2, 2 * d :].astype(jnp.float32)
    wide = own_ref[:, :d].astype(jnp.float32)
    grad = own_ref[:, d : 2 * d].astype(jnp.float32)
    recip = lax.rsqrt(jnp.mean(wide * wide, axis=-1, keepdims=True) + EPS)
    scaled = gain_ref[...] * (keep_ref[...] + got_ref[...])
    unit = wide * recip
    mean = jnp.mean(scaled * unit, axis=-1, keepdims=True)
    out_ref[0] = (grad + recip * (scaled - unit * mean)).astype(out_ref.dtype)


def on_device(sections, members, saved_in, grad_in, slot_table, gain, w_gate, w_up, w_down):
    chips = members // CORES
    r, d = grad_in.shape[1:]
    f32, bf16 = jnp.float32, jnp.bfloat16
    shape = jax.ShapeDtypeStruct
    served = [list(range(chips - CORES + c, -1, -CORES)) for c in range(CORES)]
    steps = [list(ks) for ks in zip(*served)][::-1]

    def near(i, ks):
        chip, core = divmod(i, CORES)
        k = ks[core]
        return (chip ^ k if chips & (chips - 1) == 0 else (chip + k) % chips) * CORES + core

    def to_chip(x, ks):
        return lax.ppermute(x, "seqtp", [(i, near(i, ks)) for i in range(members)])

    def to_core(x):
        return lax.ppermute(x, "seqtp", [(i, i ^ 1) for i in range(members)])

    def home(x, ks):
        pairs = [
            (s * members + near(i, ks), (s - 1) % sections * members + i)
            for s in range(sections)
            for i in range(members)
        ]
        return lax.ppermute(x, ("section", "seqtp"), pairs)

    sent, own = pl.pallas_call(
        prepare,
        out_shape=[VMEM((r, 2 * d), bf16), VMEM((r, 2 * d + d // 2), bf16)],
        in_specs=[pl.BlockSpec(memory_space=pl.ANY)] * 4,
        out_specs=whole(2),
        scratch_shapes=[
            pltpu.SMEM(slot_table.shape, slot_table.dtype),
            VMEM(saved_in.shape, bf16),
            VMEM(grad_in.shape, bf16),
            VMEM(gain.shape, bf16),
            pltpu.SemaphoreType.DMA((4,)),
        ],
        compiler_params=params(4),
        name="prepare",
    )(*[slot_table] + [pltpu.with_memory_space_constraint(x, pltpu.HBM) for x in (saved_in, grad_in, gain)])
    def stacked(parts, after=()):
        rows = sum(part.shape[0] for part in parts)
        return pl.pallas_call(
            functools.partial(stack, len(parts)),
            out_shape=VMEM((rows,) + parts[0].shape[1:], bf16),
            in_specs=whole(len(parts)) + [pl.BlockSpec(memory_space=pl.ANY)] * len(after),
            out_specs=pl.BlockSpec(memory_space=VMEM),
            compiler_params=params(4),
            name="stack",
        )(*near_core(*parts, *after))

    chip_rows = stacked([sent, to_core(sent)])
    hidden = w_down.shape[0]
    both, gate_turned = pl.pallas_call(
        fetch,
        out_shape=[VMEM((d, 2 * hidden), bf16), VMEM((hidden, d), bf16)],
        in_specs=[pl.BlockSpec(memory_space=pl.ANY)] * 2,
        out_specs=whole(2),
        scratch_shapes=[pltpu.SemaphoreType.DMA((4,)), pltpu.SemaphoreType.DMA],
        compiler_params=params(4),
        cost_estimate=pl.CostEstimate(flops=0, bytes_accessed=8 * d * hidden, transcendentals=0),
        name="fetch",
    )(*[pltpu.with_memory_space_constraint(x, pltpu.HBM) for x in (w_gate, w_up)])
    blocks = [to_chip(chip_rows, ks) for ks in steps[::-1]][::-1]
    block = stacked(blocks, [both])
    blocks = [block, to_core(block)]
    rows = block.shape[0]
    up_turned = pl.pallas_call(
        turn,
        out_shape=VMEM((hidden, d), bf16),
        in_specs=whole(1) + [pl.BlockSpec(memory_space=pl.ANY)],
        out_specs=pl.BlockSpec(memory_space=VMEM),
        compiler_params=params(4),
        cost_estimate=pl.CostEstimate(flops=0, bytes_accessed=4 * d * hidden, transcendentals=0),
        name="turn",
    )(*near_core(both, block))
    normed, grad = pl.pallas_call(
        arrange,
        out_shape=[VMEM((2 * rows, d), bf16)] * 2,
        in_specs=whole(len(blocks)),
        out_specs=whole(2),
        scratch_shapes=[VMEM((2 * rows, 2 * d), f32)],
        compiler_params=params(4),
        name="arrange",
    )(*near_core(*blocks))
    mine, other = pl.pallas_call(
        expert,
        out_shape=[VMEM((rows, d), f32)] * 2,
        in_specs=whole(5),
        out_specs=whole(2),
        compiler_params=params(16),
        name="expert",
    )(*near_core(normed, nt(grad, w_down), both, gate_turned, up_turned))
    sums = pl.pallas_call(
        add_cores,
        out_shape=[VMEM((CORES * r, d), bf16)] * len(steps),
        in_specs=whole(2),
        out_specs=whole(len(steps)),
        compiler_params=params(4),
        name="add_cores",
    )(*near_core(mine, to_core(other)))
    landed = [home(block, ks) for block, ks in zip(sums[::-1], steps[::-1])]
    own = home(own, [0] * CORES)
    keep, send = pl.pallas_call(
        add_chips,
        out_shape=[VMEM((r, d), f32)] * 2,
        in_specs=whole(len(steps)),
        out_specs=whole(2),
        compiler_params=params(4),
        name="add_chips",
    )(*near_core(*landed))
    return pl.pallas_call(
        finish,
        out_shape=shape((1, r, d), bf16),
        in_specs=whole(3),
        out_specs=pl.BlockSpec(memory_space=VMEM),
        scratch_shapes=[VMEM((1, d), f32)],
        compiler_params=params(4),
        name="finish",
    )(*near_core(own, keep, to_core(send)))


def solution(mesh):
    return jax.shard_map(
        functools.partial(on_device, mesh.shape["section"], mesh.shape["seqtp"]),
        mesh=mesh,
        in_specs=(
            P("section", None, "seqtp", None),
            P("section", "seqtp", None),
            P("section"),
            P("section", None),
            P(None, "seqtp"),
            P(None, "seqtp"),
            P("seqtp", None),
        ),
        out_specs=P("section", "seqtp", None),
        check_vma=False,
    )
```

```python
import functools

import jax
import jax.numpy as jnp
from jax import lax
from jax.experimental import pallas as pl
from jax.experimental.pallas import tpu as pltpu
from jax.sharding import PartitionSpec as P

EPS = 1e-05
CORES = 2
VMEM = pltpu.VMEM


def whole(n):
    return [pl.BlockSpec(memory_space=VMEM)] * n


def anywhere(n):
    return [pl.BlockSpec(memory_space=pl.ANY)] * n


def near_core(*arrays):
    return [pltpu.with_memory_space_constraint(x, VMEM) for x in arrays]


def far_off(*arrays):
    return [pltpu.with_memory_space_constraint(x, pltpu.HBM) for x in arrays]


def params(mib):
    return pltpu.CompilerParams(vmem_limit_bytes=mib * 2**20)


def cost(bytes_accessed):
    return pl.CostEstimate(flops=0, bytes_accessed=bytes_accessed, transcendentals=0)


def on_chip_with(bit):
    return lax.rem(lax.div(lax.axis_index("seqtp"), CORES * max(bit, 1)), 2) == 1


def crossed(blocks, swap):
    out = list(blocks)
    for n in range(0, len(blocks) - 1, 2):
        a, b = blocks[n : n + 2]
        out[n], out[n + 1] = jnp.where(swap, a, b), jnp.where(swap, b, a)
    return out


def on_first_core():
    return lax.rem(lax.axis_index("seqtp"), CORES) == 0


def nn(left, weight):
    return jnp.dot(left, weight, preferred_element_type=jnp.float32)


def nt(left, weight):
    return lax.dot_general(
        left, weight, (((1,), (1,)), ((), ())), preferred_element_type=jnp.float32
    )


def prepare(slot_ref, saved_hbm, grad_hbm, gain_hbm, sent_ref, own_ref, behind_ref, gain_ref, sems):
    r, d = grad_hbm.shape[1:]
    copies = [
        pltpu.make_async_copy(src, dst, sems.at[i])
        for i, (src, dst) in enumerate(
            (
                (saved_hbm.at[0, slot_ref[0]], behind_ref),
                (grad_hbm.at[0], sent_ref.at[:, pl.ds(d, d)]),
                (gain_hbm, gain_ref),
            )
        )
    ]
    for copy in copies:
        copy.start()
    for copy in copies:
        copy.wait()
    behind = behind_ref[...]
    wide = behind.astype(jnp.float32)
    recip = lax.rsqrt(jnp.mean(wide * wide, axis=-1, keepdims=True) + EPS)
    sent_ref[:, :d] = (wide * recip * gain_ref[...].astype(jnp.float32)).astype(jnp.bfloat16)
    own_ref[:, :d] = behind
    own_ref[:, d : 2 * d] = sent_ref[:, d:]
    piece = d // r
    for n in range(r):
        own_ref[n : n + 1, 2 * d :] = gain_ref[:, n * piece : (n + 1) * piece]


def join(mine_ref, other_ref, rows_ref):
    r = mine_ref.shape[0]
    mine, other = mine_ref[...], other_ref[...]
    first = on_first_core()
    rows_ref[:r] = jnp.where(first, mine, other)
    rows_ref[r:] = jnp.where(first, other, mine)


def fetch(gate_hbm, up_hbm, both_ref, turned_ref, sems, up_sem):
    d, h = gate_hbm.shape
    parts = sems.shape[0]
    rows = d // parts
    copies = [
        pltpu.make_async_copy(
            gate_hbm.at[pl.ds(n * rows, rows)], both_ref.at[pl.ds(n * rows, rows), pl.ds(0, h)], sems.at[n]
        )
        for n in range(parts)
    ]
    up = pltpu.make_async_copy(up_hbm, both_ref.at[:, pl.ds(h, h)], up_sem)
    for copy in copies + [up]:
        copy.start()
    for n, copy in enumerate(copies):
        copy.wait()
        turned_ref[:, n * rows : (n + 1) * rows] = both_ref[n * rows : (n + 1) * rows, :h].T
    up.wait()


def turn(both_ref, after, turned_ref):
    h, d = turned_ref.shape
    step = d // 8
    for n in range(0, d, step):
        turned_ref[:, n : n + step] = both_ref[n : n + step, h:].T


def collect(turns, own_ref, *refs):
    *blocks, after, out_ref = refs
    r = own_ref.shape[0]
    first, turned = on_first_core(), on_chip_with(turns)
    came = [ref[...] for ref in blocks[::-1]]
    nearer = [own_ref[...]] + came[:-1]
    farther = crossed(came, turned) if turns else came
    for n, (a, b) in enumerate(zip(nearer, farther)):
        out_ref[n * r : (n + 1) * r] = jnp.where(first, a, b)


def arrange(near_ref, far_ref, normed_ref, grad_ref, rows_ref):
    d = normed_ref.shape[1]
    half = near_ref.shape[0]
    first = on_first_core()
    near, far = near_ref[...].astype(jnp.float32), far_ref[...].astype(jnp.float32)
    rows_ref[:half] = jnp.where(first, near, far)
    rows_ref[half:] = jnp.where(first, far, near)
    normed_ref[...] = rows_ref[:, :d].astype(jnp.bfloat16)
    grad_ref[...] = rows_ref[:, d:].astype(jnp.bfloat16)


def expert(rows, normed_ref, hidden_ref, both_ref, gate_ref, up_ref, mine_ref, other_ref):
    h = hidden_ref.shape[1]
    gate = nn(normed_ref[...], both_ref[:, :h])
    up = nn(normed_ref[...], both_ref[:, h:])
    d_hidden = hidden_ref[...]
    p = jax.nn.sigmoid(gate)
    d_gate = d_hidden * up * p * (1.0 + gate * (1.0 - p))
    d_up = d_hidden * gate * p
    d_both = jnp.concatenate([d_gate, d_up], axis=1).astype(jnp.bfloat16)
    total = nn(d_both[:, :h], gate_ref[...]) + nn(d_both[:, h:], up_ref[...])
    first = on_first_core()
    for n in range(mine_ref.shape[0] // rows):
        even = total[2 * n * rows : (2 * n + 1) * rows]
        odd = total[(2 * n + 1) * rows : (2 * n + 2) * rows]
        mine_ref[n * rows : (n + 1) * rows] = jnp.where(first, even, odd)
        other_ref[n * rows : (n + 1) * rows] = jnp.where(first, odd, even)


def add_cores(turns, mine_ref, got_ref, *out_refs):
    total = (mine_ref[...] + got_ref[...]).astype(jnp.bfloat16)
    r = out_refs[0].shape[0]
    parts = [total[k * r : (k + 1) * r] for k in range(len(out_refs))]
    first = on_first_core()
    odd = crossed(parts, jnp.logical_not(on_chip_with(turns))) if turns else parts
    for ref, a, b in zip(out_refs, parts[::-1], odd):
        ref[...] = jnp.where(first, a, b)


def add_chips(*refs):
    *parts, keep_ref, send_ref = refs
    total = sum(ref[...].astype(jnp.float32) for ref in parts)
    r = keep_ref.shape[0]
    first = on_first_core()
    keep_ref[...] = jnp.where(first, total[:r], total[r:])
    send_ref[...] = jnp.where(first, total[r:], total[:r])


def finish(own_ref, keep_ref, got_ref, out_ref, gain_ref):
    r, d = keep_ref.shape
    piece = d // r
    for n in range(r):
        gain_ref[:, n * piece : (n + 1) * piece] = own_ref[n : n + 1, 2 * d :].astype(jnp.float32)
    wide = own_ref[:, :d].astype(jnp.float32)
    grad = own_ref[:, d : 2 * d].astype(jnp.float32)
    recip = lax.rsqrt(jnp.mean(wide * wide, axis=-1, keepdims=True) + EPS)
    scaled = gain_ref[...] * (keep_ref[...] + got_ref[...])
    unit = wide * recip
    mean = jnp.mean(scaled * unit, axis=-1, keepdims=True)
    out_ref[0] = (grad + recip * (scaled - unit * mean)).astype(out_ref.dtype)


def on_device(sections, members, saved_in, grad_in, slot_table, gain, w_gate, w_up, w_down):
    chips = members // CORES
    r, d = grad_in.shape[1:]
    hidden = w_down.shape[0]
    f32, bf16 = jnp.float32, jnp.bfloat16
    half = chips // CORES
    power = chips & (chips - 1) == 0
    out_turns, home_turns = (half, 1) if power else (0, 0)

    def swapped(n, t, bit, chip):
        return t ^ 1 if bit and chip & bit and t | 1 < n else t

    def route(goal):
        pairs = []
        for s in range(sections):
            for i in range(members):
                to, chip = goal(s, *divmod(i, CORES))
                pairs.append((s * members + i, to % sections * members + chip % chips * CORES + i % CORES))
        return pairs

    def ahead(x, t):
        def goal(s, chip, core):
            if core:
                k = half + swapped(half, t, out_turns, chip)
            else:
                k = (t + 1) % half
            return s + (k == 0), chip ^ k if power else chip + k

        return lax.ppermute(x, ("section", "seqtp"), route(goal))

    def home(x, t):
        def goal(s, chip, core):
            k = 2 * swapped(half, t, home_turns, chip) + 1 if core else 2 * (half - 1 - t)
            return s - 1, chip ^ k if power else chip - k

        return lax.ppermute(x, ("section", "seqtp"), route(goal))

    def back(x):
        return lax.ppermute(x, ("section", "seqtp"), route(lambda s, chip, core: (s - 1, chip)))

    def to_core(x):
        return lax.ppermute(x, "seqtp", [(i, i ^ 1) for i in range(members)])

    sent, own = pl.pallas_call(
        prepare,
        out_shape=[VMEM((r, 2 * d), bf16), VMEM((r, 2 * d + d // r), bf16)],
        in_specs=[pl.BlockSpec(memory_space=pltpu.SMEM)] + anywhere(3),
        out_specs=whole(2),
        scratch_shapes=[VMEM((r, d), bf16), VMEM(gain.shape, bf16), pltpu.SemaphoreType.DMA((3,))],
        compiler_params=params(4),
        name="prepare",
    )(slot_table, *far_off(saved_in, grad_in, gain))
    chip_rows = pl.pallas_call(
        join,
        out_shape=VMEM((CORES * r, 2 * d), bf16),
        in_specs=whole(2),
        out_specs=pl.BlockSpec(memory_space=VMEM),
        compiler_params=params(4),
        name="join",
    )(*near_core(sent, to_core(sent)))
    both, gate_turned = pl.pallas_call(
        fetch,
        out_shape=[VMEM((d, 2 * hidden), bf16), VMEM((hidden, d), bf16)],
        in_specs=anywhere(2),
        out_specs=whole(2),
        scratch_shapes=[pltpu.SemaphoreType.DMA((4,)), pltpu.SemaphoreType.DMA],
        compiler_params=params(4),
        cost_estimate=cost(8 * d * hidden),
        name="fetch",
    )(*far_off(w_gate, w_up))
    blocks = [ahead(chip_rows, t) for t in range(half)]
    rows = chips * r
    block = pl.pallas_call(
        functools.partial(collect, out_turns),
        out_shape=VMEM((rows, 2 * d), bf16),
        in_specs=whole(1 + len(blocks)) + anywhere(1),
        out_specs=pl.BlockSpec(memory_space=VMEM),
        compiler_params=params(4),
        name="collect",
    )(*near_core(chip_rows, *blocks[::-1], both))
    far = to_core(block)
    up_turned = pl.pallas_call(
        turn,
        out_shape=VMEM((hidden, d), bf16),
        in_specs=whole(1) + anywhere(1),
        out_specs=pl.BlockSpec(memory_space=VMEM),
        compiler_params=params(4),
        cost_estimate=cost(4 * d * hidden),
        name="turn",
    )(*near_core(both, block))
    normed, grad = pl.pallas_call(
        arrange,
        out_shape=[VMEM((2 * rows, d), bf16)] * 2,
        in_specs=whole(2),
        out_specs=whole(2),
        scratch_shapes=[VMEM((2 * rows, 2 * d), f32)],
        compiler_params=params(4),
        name="arrange",
    )(*near_core(block, far))
    mine, other = pl.pallas_call(
        functools.partial(expert, CORES * r),
        out_shape=[VMEM((rows, d), f32)] * 2,
        in_specs=whole(5),
        out_specs=whole(2),
        compiler_params=params(16),
        name="expert",
    )(*near_core(normed, nt(grad, w_down), both, gate_turned, up_turned))
    sums = pl.pallas_call(
        functools.partial(add_cores, home_turns),
        out_shape=[VMEM((CORES * r, d), bf16)] * half,
        in_specs=whole(2),
        out_specs=whole(half),
        compiler_params=params(4),
        name="add_cores",
    )(*near_core(mine, to_core(other)))
    landed = [home(x, t) for t, x in enumerate(sums)]
    own = back(own)
    keep, send = pl.pallas_call(
        add_chips,
        out_shape=[VMEM((r, d), f32)] * 2,
        in_specs=whole(half),
        out_specs=whole(2),
        compiler_params=params(4),
        name="add_chips",
    )(*near_core(*landed))
    return pl.pallas_call(
        finish,
        out_shape=jax.ShapeDtypeStruct((1, r, d), bf16),
        in_specs=whole(3),
        out_specs=pl.BlockSpec(memory_space=VMEM),
        scratch_shapes=[VMEM((1, d), f32)],
        compiler_params=params(4),
        name="finish",
    )(*near_core(own, keep, to_core(send)))


def solution(mesh):
    return jax.shard_map(
        functools.partial(on_device, mesh.shape["section"], mesh.shape["seqtp"]),
        mesh=mesh,
        in_specs=(
            P("section", None, "seqtp", None),
            P("section", "seqtp", None),
            P("section"),
            P("section", None),
            P(None, "seqtp"),
            P(None, "seqtp"),
            P("seqtp", None),
        ),
        out_specs=P("section", "seqtp", None),
        check_vma=False,
    )
```

```python
import functools

import jax
import jax.numpy as jnp
from jax import lax
from jax.experimental import pallas as pl
from jax.experimental.pallas import tpu as pltpu
from jax.sharding import PartitionSpec as P

EPS = 1e-05
CORES = 2
VMEM = pltpu.VMEM


def whole(n):
    return [pl.BlockSpec(memory_space=VMEM)] * n


def anywhere(n):
    return [pl.BlockSpec(memory_space=pl.ANY)] * n


def near_core(*arrays):
    return [pltpu.with_memory_space_constraint(x, VMEM) for x in arrays]


def far_off(*arrays):
    return [pltpu.with_memory_space_constraint(x, pltpu.HBM) for x in arrays]


def params(mib):
    return pltpu.CompilerParams(vmem_limit_bytes=mib * 2**20)


def cost(bytes_accessed):
    return pl.CostEstimate(flops=0, bytes_accessed=bytes_accessed, transcendentals=0)


def on_chip_with(bit):
    return lax.rem(lax.div(lax.axis_index("seqtp"), CORES * max(bit, 1)), 2) == 1


def crossed(blocks, swap):
    out = list(blocks)
    for n in range(0, len(blocks) - 1, 2):
        a, b = blocks[n : n + 2]
        out[n], out[n + 1] = jnp.where(swap, a, b), jnp.where(swap, b, a)
    return out


def on_first_core():
    return lax.rem(lax.axis_index("seqtp"), CORES) == 0


def nn(left, weight):
    return jnp.dot(left, weight, preferred_element_type=jnp.float32)


def nt(left, weight):
    return lax.dot_general(
        left, weight, (((1,), (1,)), ((), ())), preferred_element_type=jnp.float32
    )


def prepare(saved_hbm, grad_hbm, gain_hbm, sent_ref, raw_ref, gain_ref, sems):
    slots, r, d = saved_hbm.shape[1:]
    copies = [
        pltpu.make_async_copy(saved_hbm.at[0, n], raw_ref.at[:, pl.ds(n * d, d)], sems.at[n]) for n in range(slots)
    ]
    copies += [
        pltpu.make_async_copy(grad_hbm.at[0], sent_ref.at[:, pl.ds(slots * d, d)], sems.at[slots]),
        pltpu.make_async_copy(gain_hbm, gain_ref, sems.at[slots + 1]),
    ]
    for copy in copies:
        copy.start()
    for copy in copies:
        copy.wait()
    gain = gain_ref[...].astype(jnp.float32)
    for n in range(slots):
        wide = raw_ref[:, n * d : (n + 1) * d].astype(jnp.float32)
        recip = lax.rsqrt(jnp.mean(wide * wide, axis=-1, keepdims=True) + EPS)
        sent_ref[:, n * d : (n + 1) * d] = (wide * recip * gain).astype(jnp.bfloat16)


def join(slot_ref, mine_ref, other_ref, raw_ref, gain_ref, rows_ref, own_ref):
    r, d = mine_ref.shape[0], gain_ref.shape[1]
    first = on_first_core()
    slot = pl.ds(pl.multiple_of(slot_ref[0] * d, d), d)
    grad = pl.ds(mine_ref.shape[1] - d, d)
    for part, at in ((slot, 0), (grad, d)):
        mine, other = mine_ref[:, part], other_ref[:, part]
        rows_ref[:r, at : at + d] = jnp.where(first, mine, other)
        rows_ref[r:, at : at + d] = jnp.where(first, other, mine)
    own_ref[:, :d] = raw_ref[:, slot]
    own_ref[:, d : 2 * d] = mine_ref[:, grad]
    piece = d // r
    for n in range(r):
        own_ref[n : n + 1, 2 * d :] = gain_ref[:, n * piece : (n + 1) * piece]


def fetch(gate_hbm, up_hbm, both_ref, turned_ref, sems, up_sem):
    d, h = gate_hbm.shape
    parts = sems.shape[0]
    rows = d // parts
    copies = [
        pltpu.make_async_copy(
            gate_hbm.at[pl.ds(n * rows, rows)], both_ref.at[pl.ds(n * rows, rows), pl.ds(0, h)], sems.at[n]
        )
        for n in range(parts)
    ]
    up = pltpu.make_async_copy(up_hbm, both_ref.at[:, pl.ds(h, h)], up_sem)
    for copy in copies + [up]:
        copy.start()
    for n, copy in enumerate(copies):
        copy.wait()
        turned_ref[:, n * rows : (n + 1) * rows] = both_ref[n * rows : (n + 1) * rows, :h].T
    up.wait()


def turn(both_ref, after, turned_ref):
    h, d = turned_ref.shape
    step = d // 8
    for n in range(0, d, step):
        turned_ref[:, n : n + step] = both_ref[n : n + step, h:].T


def collect(turns, own_ref, *refs):
    *blocks, after, out_ref = refs
    r = own_ref.shape[0]
    first, turned = on_first_core(), on_chip_with(turns)
    came = [ref[...] for ref in blocks[::-1]]
    nearer = [own_ref[...]] + came[:-1]
    farther = crossed(came, turned) if turns else came
    for n, (a, b) in enumerate(zip(nearer, farther)):
        out_ref[n * r : (n + 1) * r] = jnp.where(first, a, b)


def arrange(near_ref, far_ref, normed_ref, grad_ref, rows_ref):
    d = normed_ref.shape[1]
    half = near_ref.shape[0]
    first = on_first_core()
    near, far = near_ref[...].astype(jnp.float32), far_ref[...].astype(jnp.float32)
    rows_ref[:half] = jnp.where(first, near, far)
    rows_ref[half:] = jnp.where(first, far, near)
    normed_ref[...] = rows_ref[:, :d].astype(jnp.bfloat16)
    grad_ref[...] = rows_ref[:, d:].astype(jnp.bfloat16)


def expert(rows, normed_ref, hidden_ref, both_ref, gate_ref, up_ref, mine_ref, other_ref):
    h = hidden_ref.shape[1]
    gate = nn(normed_ref[...], both_ref[:, :h])
    up = nn(normed_ref[...], both_ref[:, h:])
    d_hidden = hidden_ref[...]
    p = jax.nn.sigmoid(gate)
    d_gate = d_hidden * up * p * (1.0 + gate * (1.0 - p))
    d_up = d_hidden * gate * p
    d_both = jnp.concatenate([d_gate, d_up], axis=1).astype(jnp.bfloat16)
    total = nn(d_both[:, :h], gate_ref[...]) + nn(d_both[:, h:], up_ref[...])
    first = on_first_core()
    for n in range(mine_ref.shape[0] // rows):
        even = total[2 * n * rows : (2 * n + 1) * rows]
        odd = total[(2 * n + 1) * rows : (2 * n + 2) * rows]
        mine_ref[n * rows : (n + 1) * rows] = jnp.where(first, even, odd)
        other_ref[n * rows : (n + 1) * rows] = jnp.where(first, odd, even)


def add_cores(turns, mine_ref, got_ref, *out_refs):
    total = (mine_ref[...] + got_ref[...]).astype(jnp.bfloat16)
    r = out_refs[0].shape[0]
    parts = [total[k * r : (k + 1) * r] for k in range(len(out_refs))]
    first = on_first_core()
    odd = crossed(parts, jnp.logical_not(on_chip_with(turns))) if turns else parts
    for ref, a, b in zip(out_refs, parts[::-1], odd):
        ref[...] = jnp.where(first, a, b)


def add_chips(*refs):
    *parts, keep_ref, send_ref = refs
    total = sum(ref[...].astype(jnp.float32) for ref in parts)
    r = keep_ref.shape[0]
    first = on_first_core()
    keep_ref[...] = jnp.where(first, total[:r], total[r:])
    send_ref[...] = jnp.where(first, total[r:], total[:r])


def finish(own_ref, keep_ref, got_ref, out_ref, gain_ref):
    r, d = keep_ref.shape
    piece = d // r
    for n in range(r):
        gain_ref[:, n * piece : (n + 1) * piece] = own_ref[n : n + 1, 2 * d :].astype(jnp.float32)
    wide = own_ref[:, :d].astype(jnp.float32)
    grad = own_ref[:, d : 2 * d].astype(jnp.float32)
    recip = lax.rsqrt(jnp.mean(wide * wide, axis=-1, keepdims=True) + EPS)
    scaled = gain_ref[...] * (keep_ref[...] + got_ref[...])
    unit = wide * recip
    mean = jnp.mean(scaled * unit, axis=-1, keepdims=True)
    out_ref[0] = (grad + recip * (scaled - unit * mean)).astype(out_ref.dtype)


def on_device(sections, members, saved_in, grad_in, slot_table, gain, w_gate, w_up, w_down):
    chips = members // CORES
    r, d = grad_in.shape[1:]
    hidden = w_down.shape[0]
    f32, bf16 = jnp.float32, jnp.bfloat16
    half = chips // CORES
    power = chips & (chips - 1) == 0
    out_turns, home_turns = (half, 1) if power else (0, 0)

    def swapped(n, t, bit, chip):
        return t ^ 1 if bit and chip & bit and t | 1 < n else t

    def route(goal):
        pairs = []
        for s in range(sections):
            for i in range(members):
                to, chip = goal(s, *divmod(i, CORES))
                pairs.append((s * members + i, to % sections * members + chip % chips * CORES + i % CORES))
        return pairs

    def ahead(x, t):
        def goal(s, chip, core):
            if core:
                k = half + swapped(half, t, out_turns, chip)
            else:
                k = (t + 1) % half
            aside = s if k else s ^ 1 if sections % 2 == 0 else s + 1
            return aside, chip ^ k if power else chip + k

        return lax.ppermute(x, ("section", "seqtp"), route(goal))

    def home(x, t):
        def goal(s, chip, core):
            k = 2 * swapped(half, t, home_turns, chip) + 1 if core else 2 * (half - 1 - t)
            return s - 1, chip ^ k if power else chip - k

        return lax.ppermute(x, ("section", "seqtp"), route(goal))

    def back(x):
        return lax.ppermute(x, ("section", "seqtp"), route(lambda s, chip, core: (s - 1, chip)))

    def to_core(x):
        return lax.ppermute(x, "seqtp", [(i, i ^ 1) for i in range(members)])

    slots = saved_in.shape[1]
    sent, raw, gain_row = pl.pallas_call(
        prepare,
        out_shape=[VMEM((r, (slots + 1) * d), bf16), VMEM((r, slots * d), bf16), VMEM(gain.shape, bf16)],
        in_specs=anywhere(3),
        out_specs=whole(3),
        scratch_shapes=[pltpu.SemaphoreType.DMA((slots + 2,))],
        compiler_params=params(4),
        name="prepare",
    )(*far_off(saved_in, grad_in, gain))
    chip_rows, own = pl.pallas_call(
        join,
        out_shape=[VMEM((CORES * r, 2 * d), bf16), VMEM((r, 2 * d + d // r), bf16)],
        in_specs=[pl.BlockSpec(memory_space=pltpu.SMEM)] + whole(4),
        out_specs=whole(2),
        compiler_params=params(4),
        name="join",
    )(slot_table, *near_core(sent, to_core(sent), raw, gain_row))
    both, gate_turned = pl.pallas_call(
        fetch,
        out_shape=[VMEM((d, 2 * hidden), bf16), VMEM((hidden, d), bf16)],
        in_specs=anywhere(2),
        out_specs=whole(2),
        scratch_shapes=[pltpu.SemaphoreType.DMA((4,)), pltpu.SemaphoreType.DMA],
        compiler_params=params(4),
        cost_estimate=cost(8 * d * hidden),
        name="fetch",
    )(*far_off(w_gate, w_up))
    blocks = [ahead(chip_rows, t) for t in range(half)]
    rows = chips * r
    block = pl.pallas_call(
        functools.partial(collect, out_turns),
        out_shape=VMEM((rows, 2 * d), bf16),
        in_specs=whole(1 + len(blocks)) + anywhere(1),
        out_specs=pl.BlockSpec(memory_space=VMEM),
        compiler_params=params(4),
        name="collect",
    )(*near_core(chip_rows, *blocks[::-1], both))
    far = to_core(block)
    up_turned = pl.pallas_call(
        turn,
        out_shape=VMEM((hidden, d), bf16),
        in_specs=whole(1) + anywhere(1),
        out_specs=pl.BlockSpec(memory_space=VMEM),
        compiler_params=params(4),
        cost_estimate=cost(4 * d * hidden),
        name="turn",
    )(*near_core(both, block))
    normed, grad = pl.pallas_call(
        arrange,
        out_shape=[VMEM((2 * rows, d), bf16)] * 2,
        in_specs=whole(2),
        out_specs=whole(2),
        scratch_shapes=[VMEM((2 * rows, 2 * d), f32)],
        compiler_params=params(4),
        name="arrange",
    )(*near_core(block, far))
    mine, other = pl.pallas_call(
        functools.partial(expert, CORES * r),
        out_shape=[VMEM((rows, d), f32)] * 2,
        in_specs=whole(5),
        out_specs=whole(2),
        compiler_params=params(16),
        name="expert",
    )(*near_core(normed, nt(grad, w_down), both, gate_turned, up_turned))
    sums = pl.pallas_call(
        functools.partial(add_cores, home_turns),
        out_shape=[VMEM((CORES * r, d), bf16)] * half,
        in_specs=whole(2),
        out_specs=whole(half),
        compiler_params=params(4),
        name="add_cores",
    )(*near_core(mine, to_core(other)))
    landed = [home(x, t) for t, x in enumerate(sums)]
    own = back(own)
    keep, send = pl.pallas_call(
        add_chips,
        out_shape=[VMEM((r, d), f32)] * 2,
        in_specs=whole(half),
        out_specs=whole(2),
        compiler_params=params(4),
        name="add_chips",
    )(*near_core(*landed))
    return pl.pallas_call(
        finish,
        out_shape=jax.ShapeDtypeStruct((1, r, d), bf16),
        in_specs=whole(3),
        out_specs=pl.BlockSpec(memory_space=VMEM),
        scratch_shapes=[VMEM((1, d), f32)],
        compiler_params=params(4),
        name="finish",
    )(*near_core(own, keep, to_core(send)))


def solution(mesh):
    return jax.shard_map(
        functools.partial(on_device, mesh.shape["section"], mesh.shape["seqtp"]),
        mesh=mesh,
        in_specs=(
            P("section", None, "seqtp", None),
            P("section", "seqtp", None),
            P("section"),
            P("section", None),
            P(None, "seqtp"),
            P(None, "seqtp"),
            P("seqtp", None),
        ),
        out_specs=P("section", "seqtp", None),
        check_vma=False,
    )
```

```python
import functools

import jax
import jax.numpy as jnp
from jax import lax
from jax.experimental import pallas as pl
from jax.experimental.pallas import tpu as pltpu
from jax.sharding import PartitionSpec as P

EPS = 1e-05
CORES = 2
VMEM = pltpu.VMEM


def whole(n):
    return [pl.BlockSpec(memory_space=VMEM)] * n


def anywhere(n):
    return [pl.BlockSpec(memory_space=pl.ANY)] * n


def near_core(*arrays):
    return [pltpu.with_memory_space_constraint(x, VMEM) for x in arrays]


def far_off(*arrays):
    return [pltpu.with_memory_space_constraint(x, pltpu.HBM) for x in arrays]


def params(mib):
    return pltpu.CompilerParams(vmem_limit_bytes=mib * 2**20)


def cost(bytes_accessed):
    return pl.CostEstimate(flops=0, bytes_accessed=bytes_accessed, transcendentals=0)


def on_chip_with(bit):
    return lax.rem(lax.div(lax.axis_index("seqtp"), CORES * max(bit, 1)), 2) == 1


def crossed(blocks, swap):
    out = list(blocks)
    for n in range(0, len(blocks) - 1, 2):
        a, b = blocks[n : n + 2]
        out[n], out[n + 1] = jnp.where(swap, a, b), jnp.where(swap, b, a)
    return out


def on_first_core():
    return lax.rem(lax.axis_index("seqtp"), CORES) == 0


def nn(left, weight):
    return jnp.dot(left, weight, preferred_element_type=jnp.float32)


def nt(left, weight):
    return lax.dot_general(
        left, weight, (((1,), (1,)), ((), ())), preferred_element_type=jnp.float32
    )


def prepare(saved_hbm, grad_hbm, gain_hbm, sent_ref, gain_ref, sems):
    slots, r, d = saved_hbm.shape[1:]
    copies = [
        pltpu.make_async_copy(saved_hbm.at[0, n], sent_ref.at[:, pl.ds(n * d, d)], sems.at[n]) for n in range(slots)
    ]
    copies += [
        pltpu.make_async_copy(grad_hbm.at[0], sent_ref.at[:, pl.ds(slots * d, d)], sems.at[slots]),
        pltpu.make_async_copy(gain_hbm, gain_ref, sems.at[slots + 1]),
    ]
    for copy in copies:
        copy.start()
    for copy in copies:
        copy.wait()


def join(slot_ref, mine_ref, other_ref, gain_ref, rows_ref):
    r, d = mine_ref.shape[0], gain_ref.shape[1]
    first = on_first_core()
    slot = pl.ds(pl.multiple_of(slot_ref[0] * d, d), d)
    grad = pl.ds(mine_ref.shape[1] - d, d)
    for part, at in ((slot, 0), (grad, d)):
        mine, other = mine_ref[:, part], other_ref[:, part]
        rows_ref[:r, at : at + d] = jnp.where(first, mine, other)
        rows_ref[r:, at : at + d] = jnp.where(first, other, mine)
    piece = rows_ref.shape[1] - 2 * d
    for n in range(rows_ref.shape[0]):
        rows_ref[n : n + 1, 2 * d :] = gain_ref[:, n * piece : (n + 1) * piece]


def fetch(gate_hbm, up_hbm, both_ref, turned_ref, sems, up_sem):
    d, h = gate_hbm.shape
    parts = sems.shape[0]
    rows = d // parts
    copies = [
        pltpu.make_async_copy(
            gate_hbm.at[pl.ds(n * rows, rows)], both_ref.at[pl.ds(n * rows, rows), pl.ds(0, h)], sems.at[n]
        )
        for n in range(parts)
    ]
    up = pltpu.make_async_copy(up_hbm, both_ref.at[:, pl.ds(h, h)], up_sem)
    for copy in copies + [up]:
        copy.start()
    for n, copy in enumerate(copies):
        copy.wait()
        turned_ref[:, n * rows : (n + 1) * rows] = both_ref[n * rows : (n + 1) * rows, :h].T
    up.wait()


def turn(both_ref, after, turned_ref):
    h, d = turned_ref.shape
    step = d // 8
    for n in range(0, d, step):
        turned_ref[:, n : n + step] = both_ref[n : n + step, h:].T


def collect(turns, *refs):
    *blocks, after, out_ref, gain_ref = refs
    r = blocks[0].shape[0]
    first, turned = on_first_core(), on_chip_with(turns)
    came = [ref[:, : out_ref.shape[1]] for ref in blocks]
    nearer = came[-1:] + came[:-1]
    farther = crossed(came, turned) if turns else came
    for n, (a, b) in enumerate(zip(nearer, farther)):
        out_ref[n * r : (n + 1) * r] = jnp.where(first, a, b)
    width = out_ref.shape[1]
    piece = blocks[0].shape[1] - width
    for n in range(r):
        gain_ref[:, n * piece : (n + 1) * piece] = blocks[0][n : n + 1, width:].astype(jnp.float32)


def arrange(near_ref, far_ref, gain_ref, normed_ref, grad_ref, own_ref, rows_ref):
    d = normed_ref.shape[1]
    half, r = near_ref.shape[0], own_ref.shape[0]
    first = on_first_core()
    near, far = near_ref[...].astype(jnp.float32), far_ref[...].astype(jnp.float32)
    rows_ref[:half] = jnp.where(first, near, far)
    rows_ref[half:] = jnp.where(first, far, near)
    grad_ref[...] = rows_ref[:, d:].astype(jnp.bfloat16)
    wide = rows_ref[:, :d]
    recip = lax.rsqrt(jnp.mean(wide * wide, axis=-1, keepdims=True) + EPS)
    normed_ref[...] = (wide * recip * gain_ref[...]).astype(jnp.bfloat16)
    own_ref[:, : 2 * d] = jnp.where(first, rows_ref[:r], rows_ref[r : 2 * r]).astype(jnp.bfloat16)
    piece = d // r
    for n in range(r):
        own_ref[n : n + 1, 2 * d :] = gain_ref[:, n * piece : (n + 1) * piece].astype(jnp.bfloat16)


def expert(rows, normed_ref, hidden_ref, both_ref, gate_ref, up_ref, mine_ref, other_ref):
    h = hidden_ref.shape[1]
    gate = nn(normed_ref[...], both_ref[:, :h])
    up = nn(normed_ref[...], both_ref[:, h:])
    d_hidden = hidden_ref[...]
    p = jax.nn.sigmoid(gate)
    d_gate = d_hidden * up * p * (1.0 + gate * (1.0 - p))
    d_up = d_hidden * gate * p
    d_both = jnp.concatenate([d_gate, d_up], axis=1).astype(jnp.bfloat16)
    total = nn(d_both[:, :h], gate_ref[...]) + nn(d_both[:, h:], up_ref[...])
    first = on_first_core()
    for n in range(mine_ref.shape[0] // rows):
        even = total[2 * n * rows : (2 * n + 1) * rows]
        odd = total[(2 * n + 1) * rows : (2 * n + 2) * rows]
        mine_ref[n * rows : (n + 1) * rows] = jnp.where(first, even, odd)
        other_ref[n * rows : (n + 1) * rows] = jnp.where(first, odd, even)


def add_cores(turns, mine_ref, got_ref, *out_refs):
    total = (mine_ref[...] + got_ref[...]).astype(jnp.bfloat16)
    r = out_refs[0].shape[0]
    parts = [total[k * r : (k + 1) * r] for k in range(len(out_refs))]
    first = on_first_core()
    odd = crossed(parts, jnp.logical_not(on_chip_with(turns))) if turns else parts
    for ref, a, b in zip(out_refs, parts[::-1], odd):
        ref[...] = jnp.where(first, a, b)


def add_chips(stays, local_ref, *refs):
    *parts, keep_ref, send_ref = refs
    first = on_first_core()
    stayed = jnp.logical_and(first, stays(lax.axis_index("section")))
    total = jnp.where(stayed, local_ref[...], parts[-1][...]).astype(jnp.float32)
    for ref in parts[:-1]:
        total = total + ref[...].astype(jnp.float32)
    r = keep_ref.shape[0]
    keep_ref[...] = jnp.where(first, total[:r], total[r:])
    send_ref[...] = jnp.where(first, total[r:], total[:r])


def finish(stays, stayed_ref, moved_ref, keep_ref, got_ref, out_ref, gain_ref):
    r, d = keep_ref.shape
    here = stays(lax.axis_index("section"))
    own = jnp.where(here, stayed_ref[...].astype(jnp.float32), moved_ref[...].astype(jnp.float32))
    piece = d // r
    for n in range(r):
        gain_ref[:, n * piece : (n + 1) * piece] = own[n : n + 1, 2 * d :]
    wide, grad = own[:, :d], own[:, d : 2 * d]
    recip = lax.rsqrt(jnp.mean(wide * wide, axis=-1, keepdims=True) + EPS)
    scaled = gain_ref[...] * (keep_ref[...] + got_ref[...])
    unit = wide * recip
    mean = jnp.mean(scaled * unit, axis=-1, keepdims=True)
    out_ref[0] = (grad + recip * (scaled - unit * mean)).astype(out_ref.dtype)


def on_device(sections, members, saved_in, grad_in, slot_table, gain, w_gate, w_up, w_down):
    chips = members // CORES
    r, d = grad_in.shape[1:]
    hidden = w_down.shape[0]
    f32, bf16 = jnp.float32, jnp.bfloat16
    half = chips // CORES
    power = chips & (chips - 1) == 0
    out_turns, home_turns = (half, 1) if power else (0, 0)

    def swapped(n, t, bit, chip):
        return t ^ 1 if bit and chip & bit and t | 1 < n else t

    def route(goal):
        pairs = []
        for s in range(sections):
            for i in range(members):
                to, chip = goal(s, *divmod(i, CORES))
                pairs.append((s * members + i, to % sections * members + chip % chips * CORES + i % CORES))
        return pairs

    even = sections % 2 == 0

    def beside(s):
        return s ^ 1 if even else s - 1

    def before(s):
        return s - 2 * (s % 2) if even else s

    def stays(section):
        return lax.rem(section, 2) == 0 if even else section >= 0

    def ahead(x, t):
        def goal(s, chip, core):
            k = half + swapped(half, t, out_turns, chip) if core else (t + 1) % half
            return beside(s), chip ^ k if power else chip + k

        return lax.ppermute(x, ("section", "seqtp"), route(goal))

    def home(x, t):
        def goal(s, chip, core):
            k = 2 * swapped(half, t, home_turns, chip) + 1 if core else 2 * (half - 1 - t)
            to = before(s) if k else s - 2 if even else s - 1
            return to, chip ^ k if power else chip - k

        return lax.ppermute(x, ("section", "seqtp"), route(goal))

    def back(x):
        return lax.ppermute(x, ("section", "seqtp"), route(lambda s, chip, core: (s - 2 if even else s - 1, chip)))

    def to_core(x):
        return lax.ppermute(x, "seqtp", [(i, i ^ 1) for i in range(members)])

    slots = saved_in.shape[1]
    sent, gain_row = pl.pallas_call(
        prepare,
        out_shape=[VMEM((r, (slots + 1) * d), bf16), VMEM(gain.shape, bf16)],
        in_specs=anywhere(3),
        out_specs=whole(2),
        scratch_shapes=[pltpu.SemaphoreType.DMA((slots + 2,))],
        compiler_params=params(4),
        name="prepare",
    )(*far_off(saved_in, grad_in, gain))
    chip_rows = pl.pallas_call(
        join,
        out_shape=VMEM((CORES * r, 2 * d + d // (CORES * r)), bf16),
        in_specs=[pl.BlockSpec(memory_space=pltpu.SMEM)] + whole(3),
        out_specs=pl.BlockSpec(memory_space=VMEM),
        compiler_params=params(4),
        name="join",
    )(slot_table, *near_core(sent, to_core(sent), gain_row))
    both, gate_turned = pl.pallas_call(
        fetch,
        out_shape=[VMEM((d, 2 * hidden), bf16), VMEM((hidden, d), bf16)],
        in_specs=anywhere(2),
        out_specs=whole(2),
        scratch_shapes=[pltpu.SemaphoreType.DMA((4,)), pltpu.SemaphoreType.DMA],
        compiler_params=params(4),
        cost_estimate=cost(8 * d * hidden),
        name="fetch",
    )(*far_off(w_gate, w_up))
    blocks = [ahead(chip_rows, t) for t in range(half)]
    rows = chips * r
    block, gain_wide = pl.pallas_call(
        functools.partial(collect, out_turns),
        out_shape=[VMEM((rows, 2 * d), bf16), VMEM((1, d), f32)],
        in_specs=whole(len(blocks)) + anywhere(1),
        out_specs=whole(2),
        compiler_params=params(4),
        name="collect",
    )(*near_core(*blocks, both))
    far = to_core(block)
    up_turned = pl.pallas_call(
        turn,
        out_shape=VMEM((hidden, d), bf16),
        in_specs=whole(1) + anywhere(1),
        out_specs=pl.BlockSpec(memory_space=VMEM),
        compiler_params=params(4),
        cost_estimate=cost(4 * d * hidden),
        name="turn",
    )(*near_core(both, block))
    normed, grad, own = pl.pallas_call(
        arrange,
        out_shape=[VMEM((2 * rows, d), bf16)] * 2 + [VMEM((r, 2 * d + d // r), bf16)],
        in_specs=whole(3),
        out_specs=whole(3),
        scratch_shapes=[VMEM((2 * rows, 2 * d), f32)],
        compiler_params=params(16),
        name="arrange",
    )(*near_core(block, far, gain_wide))
    mine, other = pl.pallas_call(
        functools.partial(expert, CORES * r),
        out_shape=[VMEM((rows, d), f32)] * 2,
        in_specs=whole(5),
        out_specs=whole(2),
        compiler_params=params(16),
        name="expert",
    )(*near_core(normed, nt(grad, w_down), both, gate_turned, up_turned))
    sums = pl.pallas_call(
        functools.partial(add_cores, home_turns),
        out_shape=[VMEM((CORES * r, d), bf16)] * half,
        in_specs=whole(2),
        out_specs=whole(half),
        compiler_params=params(4),
        name="add_cores",
    )(*near_core(mine, to_core(other)))
    landed = [home(x, t) for t, x in enumerate(sums)]
    moved = back(own)
    keep, send = pl.pallas_call(
        functools.partial(add_chips, stays),
        out_shape=[VMEM((r, d), f32)] * 2,
        in_specs=whole(1 + half),
        out_specs=whole(2),
        compiler_params=params(4),
        name="add_chips",
    )(*near_core(sums[-1], *landed))
    return pl.pallas_call(
        functools.partial(finish, stays),
        out_shape=jax.ShapeDtypeStruct((1, r, d), bf16),
        in_specs=whole(4),
        out_specs=pl.BlockSpec(memory_space=VMEM),
        scratch_shapes=[VMEM((1, d), f32)],
        compiler_params=params(4),
        name="finish",
    )(*near_core(own, moved, keep, to_core(send)))


def solution(mesh):
    return jax.shard_map(
        functools.partial(on_device, mesh.shape["section"], mesh.shape["seqtp"]),
        mesh=mesh,
        in_specs=(
            P("section", None, "seqtp", None),
            P("section", "seqtp", None),
            P("section"),
            P("section", None),
            P(None, "seqtp"),
            P(None, "seqtp"),
            P("seqtp", None),
        ),
        out_specs=P("section", "seqtp", None),
        check_vma=False,
    )
```

```python
import functools

import jax
import jax.numpy as jnp
from jax import lax
from jax.experimental import pallas as pl
from jax.experimental.pallas import tpu as pltpu
from jax.sharding import PartitionSpec as P

EPS = 1e-05
CORES = 2
VMEM = pltpu.VMEM


def whole(n):
    return [pl.BlockSpec(memory_space=VMEM)] * n


def anywhere(n):
    return [pl.BlockSpec(memory_space=pl.ANY)] * n


def near_core(*arrays):
    return [pltpu.with_memory_space_constraint(x, VMEM) for x in arrays]


def far_off(*arrays):
    return [pltpu.with_memory_space_constraint(x, pltpu.HBM) for x in arrays]


def params(mib):
    return pltpu.CompilerParams(vmem_limit_bytes=mib * 2**20)


def cost(bytes_accessed):
    return pl.CostEstimate(flops=0, bytes_accessed=bytes_accessed, transcendentals=0)


def on_chip_with(bit):
    return lax.rem(lax.div(lax.axis_index("seqtp"), CORES * max(bit, 1)), 2) == 1


def crossed(blocks, swap):
    out = list(blocks)
    for n in range(0, len(blocks) - 1, 2):
        a, b = blocks[n : n + 2]
        out[n], out[n + 1] = jnp.where(swap, a, b), jnp.where(swap, b, a)
    return out


def on_first_core():
    return lax.rem(lax.axis_index("seqtp"), CORES) == 0


def nn(left, weight):
    return jnp.dot(left, weight, preferred_element_type=jnp.float32)


def prepare(saved_hbm, grad_hbm, gain_hbm, sent_ref, gain_ref, sems):
    slots, r, d = saved_hbm.shape[1:]
    copies = [
        pltpu.make_async_copy(saved_hbm.at[0, n], sent_ref.at[:, pl.ds(n * d, d)], sems.at[n]) for n in range(slots)
    ]
    copies += [
        pltpu.make_async_copy(grad_hbm.at[0], sent_ref.at[:, pl.ds(slots * d, d)], sems.at[slots]),
        pltpu.make_async_copy(gain_hbm, gain_ref, sems.at[slots + 1]),
    ]
    for copy in copies:
        copy.start()
    for copy in copies:
        copy.wait()


def join(slot_ref, mine_ref, other_ref, gain_ref, rows_ref):
    r, d = mine_ref.shape[0], gain_ref.shape[1]
    first = on_first_core()
    slot = pl.ds(pl.multiple_of(slot_ref[0] * d, d), d)
    grad = pl.ds(mine_ref.shape[1] - d, d)
    for part, at in ((slot, 0), (grad, d)):
        mine, other = mine_ref[:, part], other_ref[:, part]
        rows_ref[:r, at : at + d] = jnp.where(first, mine, other)
        rows_ref[r:, at : at + d] = jnp.where(first, other, mine)
    piece = rows_ref.shape[1] - 2 * d
    for n in range(rows_ref.shape[0]):
        rows_ref[n : n + 1, 2 * d :] = gain_ref[:, n * piece : (n + 1) * piece]


def fetch(gate_hbm, up_hbm, down_hbm, both_ref, gate_ref, up_ref, down_ref, sems, last_sem):
    d, h = gate_hbm.shape
    parts = sems.shape[1]
    rows = d // parts
    columns = (gate_hbm, up_hbm)
    copies = [
        [
            pltpu.make_async_copy(
                src.at[pl.ds(n * rows, rows)], both_ref.at[pl.ds(n * rows, rows), pl.ds(k * h, h)], sems.at[k, n]
            )
            for n in range(parts)
        ]
        for k, src in enumerate(columns)
    ]
    last = pltpu.make_async_copy(down_hbm, down_ref, last_sem)
    for copy in copies[0] + copies[1] + [last]:
        copy.start()
    for k, turned_ref in enumerate((gate_ref, up_ref)):
        for n, copy in enumerate(copies[k]):
            copy.wait()
            here = slice(n * rows, (n + 1) * rows)
            turned_ref[:, here] = both_ref[here, k * h : (k + 1) * h].T
    last.wait()


def turn(down_ref, after, turned_ref):
    d = turned_ref.shape[0]
    step = d // 8
    for n in range(0, d, step):
        turned_ref[n : n + step] = down_ref[:, n : n + step].T


def collect(turns, *refs):
    *blocks, after, out_ref, gain_ref = refs
    r = blocks[0].shape[0]
    first, turned = on_first_core(), on_chip_with(turns)
    came = [ref[:, : out_ref.shape[1]] for ref in blocks[::-1]]
    nearer = came[-1:] + came[:-1]
    farther = crossed(came, turned) if turns else came
    for n, (a, b) in enumerate(zip(nearer, farther)):
        out_ref[n * r : (n + 1) * r] = jnp.where(first, a, b)
    width = out_ref.shape[1]
    piece = blocks[0].shape[1] - width
    for n in range(r):
        gain_ref[:, n * piece : (n + 1) * piece] = blocks[0][n : n + 1, width:].astype(jnp.float32)


def arrange(near_ref, far_ref, gain_ref, normed_ref, grad_ref, own_ref, rows_ref):
    d = normed_ref.shape[1]
    half, r = near_ref.shape[0], own_ref.shape[0]
    first = on_first_core()
    near, far = near_ref[...].astype(jnp.float32), far_ref[...].astype(jnp.float32)
    rows_ref[:half] = jnp.where(first, near, far)
    rows_ref[half:] = jnp.where(first, far, near)
    grad_ref[...] = rows_ref[:, d:].astype(jnp.bfloat16)
    wide = rows_ref[:, :d]
    recip = lax.rsqrt(jnp.mean(wide * wide, axis=-1, keepdims=True) + EPS)
    normed_ref[...] = (wide * recip * gain_ref[...]).astype(jnp.bfloat16)
    own_ref[:, : 2 * d] = jnp.where(first, rows_ref[:r], rows_ref[r : 2 * r]).astype(jnp.bfloat16)
    piece = d // r
    for n in range(r):
        own_ref[n : n + 1, 2 * d :] = gain_ref[:, n * piece : (n + 1) * piece].astype(jnp.bfloat16)


def expert(rows, normed_ref, grad_ref, both_ref, gate_ref, up_ref, down_ref, mine_ref, other_ref):
    h = down_ref.shape[1]
    both = nn(normed_ref[...], both_ref[...])
    gate, up = both[:, :h], both[:, h:]
    d_hidden = nn(grad_ref[...], down_ref[...])
    p = jax.nn.sigmoid(gate)
    d_gate = d_hidden * up * p * (1.0 + gate * (1.0 - p))
    d_up = d_hidden * gate * p
    d_both = jnp.concatenate([d_gate, d_up], axis=1).astype(jnp.bfloat16)
    total = nn(d_both[:, :h], gate_ref[...]) + nn(d_both[:, h:], up_ref[...])
    first = on_first_core()
    for n in range(mine_ref.shape[0] // rows):
        even = total[2 * n * rows : (2 * n + 1) * rows]
        odd = total[(2 * n + 1) * rows : (2 * n + 2) * rows]
        mine_ref[n * rows : (n + 1) * rows] = jnp.where(first, even, odd)
        other_ref[n * rows : (n + 1) * rows] = jnp.where(first, odd, even)


def add_cores(turns, mine_ref, got_ref, *out_refs):
    total = (mine_ref[...] + got_ref[...]).astype(jnp.bfloat16)
    r = out_refs[0].shape[0]
    parts = [total[k * r : (k + 1) * r] for k in range(len(out_refs))]
    first = on_first_core()
    odd = crossed(parts, jnp.logical_not(on_chip_with(turns))) if turns else parts
    for ref, a, b in zip(out_refs, parts[::-1], odd):
        ref[...] = jnp.where(first, a, b)


def add_chips(stays, local_ref, *refs):
    *parts, keep_ref, send_ref = refs
    first = on_first_core()
    stayed = jnp.logical_and(first, stays(lax.axis_index("section")))
    total = jnp.where(stayed, local_ref[...], parts[-1][...]).astype(jnp.float32)
    for ref in parts[:-1]:
        total = total + ref[...].astype(jnp.float32)
    r = keep_ref.shape[0]
    keep_ref[...] = jnp.where(first, total[:r], total[r:])
    send_ref[...] = jnp.where(first, total[r:], total[:r])


def finish(stays, stayed_ref, moved_ref, keep_ref, got_ref, out_ref, gain_ref):
    r, d = keep_ref.shape
    here = stays(lax.axis_index("section"))
    own = jnp.where(here, stayed_ref[...].astype(jnp.float32), moved_ref[...].astype(jnp.float32))
    piece = d // r
    for n in range(r):
        gain_ref[:, n * piece : (n + 1) * piece] = own[n : n + 1, 2 * d :]
    wide, grad = own[:, :d], own[:, d : 2 * d]
    recip = lax.rsqrt(jnp.mean(wide * wide, axis=-1, keepdims=True) + EPS)
    scaled = gain_ref[...] * (keep_ref[...] + got_ref[...])
    unit = wide * recip
    mean = jnp.mean(scaled * unit, axis=-1, keepdims=True)
    out_ref[0] = (grad + recip * (scaled - unit * mean)).astype(out_ref.dtype)


def on_device(sections, members, saved_in, grad_in, slot_table, gain, w_gate, w_up, w_down):
    chips = members // CORES
    r, d = grad_in.shape[1:]
    hidden = w_down.shape[0]
    f32, bf16 = jnp.float32, jnp.bfloat16
    half = chips // CORES
    power = chips & (chips - 1) == 0
    out_turns, home_turns = (half, 1) if power else (0, 0)

    def swapped(n, t, bit, chip):
        return t ^ 1 if bit and chip & bit and t | 1 < n else t

    def route(goal):
        pairs = []
        for s in range(sections):
            for i in range(members):
                to, chip, *core = goal(s, *divmod(i, CORES))
                core = core[0] if core else i % CORES
                pairs.append((s * members + i, to % sections * members + chip % chips * CORES + core))
        return pairs

    even = sections % 2 == 0

    def beside(s):
        return s ^ 1 if even else s - 1

    def before(s):
        return s - 2 * (s % 2) if even else s

    def stays(section):
        return lax.rem(section, 2) == 0 if even else section >= 0

    def ahead(x, t):
        def goal(s, chip, core):
            k = half + swapped(half, t, out_turns, chip) if core else (t + 1) % half
            return beside(s), chip ^ k if power else chip + k

        return lax.ppermute(x, ("section", "seqtp"), route(goal))

    def home(x, t):
        def goal(s, chip, core):
            k = 2 * swapped(half, t, home_turns, chip) + 1 if core else 2 * (half - 1 - t)
            to = before(s) if k else s - 2 if even else s - 1
            return to, chip ^ k if power else chip - k

        return lax.ppermute(x, ("section", "seqtp"), route(goal))

    def back(x):
        return lax.ppermute(x, ("section", "seqtp"), route(lambda s, chip, core: (s, chip, core ^ 1) if before(s) == s else (before(s), chip)))

    def to_core(x):
        return lax.ppermute(x, "seqtp", [(i, i ^ 1) for i in range(members)])

    slots = saved_in.shape[1]
    sent, gain_row = pl.pallas_call(
        prepare,
        out_shape=[VMEM((r, (slots + 1) * d), bf16), VMEM(gain.shape, bf16)],
        in_specs=anywhere(3),
        out_specs=whole(2),
        scratch_shapes=[pltpu.SemaphoreType.DMA((slots + 2,))],
        compiler_params=params(4),
        name="prepare",
    )(*far_off(saved_in, grad_in, gain))
    chip_rows = pl.pallas_call(
        join,
        out_shape=VMEM((CORES * r, 2 * d + d // (CORES * r)), bf16),
        in_specs=[pl.BlockSpec(memory_space=pltpu.SMEM)] + whole(3),
        out_specs=pl.BlockSpec(memory_space=VMEM),
        compiler_params=params(4),
        name="join",
    )(slot_table, *near_core(sent, to_core(sent), gain_row))
    both, gate_turned, up_turned, down = pl.pallas_call(
        fetch,
        out_shape=[VMEM((d, 2 * hidden), bf16)] + [VMEM((hidden, d), bf16)] * 3,
        in_specs=anywhere(3),
        out_specs=whole(4),
        scratch_shapes=[pltpu.SemaphoreType.DMA((2, 4)), pltpu.SemaphoreType.DMA],
        compiler_params=params(4),
        cost_estimate=cost(12 * d * hidden),
        name="fetch",
    )(*far_off(w_gate, w_up, w_down))
    blocks = [ahead(chip_rows, t) for t in range(half)]
    rows = chips * r
    block, gain_wide = pl.pallas_call(
        functools.partial(collect, out_turns),
        out_shape=[VMEM((rows, 2 * d), bf16), VMEM((1, d), f32)],
        in_specs=whole(len(blocks)) + anywhere(1),
        out_specs=whole(2),
        compiler_params=params(4),
        name="collect",
    )(*near_core(*blocks[::-1], both))
    far = to_core(block)
    down_turned = pl.pallas_call(
        turn,
        out_shape=VMEM((d, hidden), bf16),
        in_specs=whole(1) + anywhere(1),
        out_specs=pl.BlockSpec(memory_space=VMEM),
        compiler_params=params(4),
        cost_estimate=cost(4 * d * hidden),
        name="turn",
    )(*near_core(down, block))
    normed, grad, own = pl.pallas_call(
        arrange,
        out_shape=[VMEM((2 * rows, d), bf16)] * 2 + [VMEM((r, 2 * d + d // r), bf16)],
        in_specs=whole(3),
        out_specs=whole(3),
        scratch_shapes=[VMEM((2 * rows, 2 * d), f32)],
        compiler_params=params(16),
        name="arrange",
    )(*near_core(block, far, gain_wide))
    mine, other = pl.pallas_call(
        functools.partial(expert, CORES * r),
        out_shape=[VMEM((rows, d), f32)] * 2,
        in_specs=whole(6),
        out_specs=whole(2),
        compiler_params=params(16),
        name="expert",
    )(*near_core(normed, grad, both, gate_turned, up_turned, down_turned))
    sums = pl.pallas_call(
        functools.partial(add_cores, home_turns),
        out_shape=[VMEM((CORES * r, d), bf16)] * half,
        in_specs=whole(2),
        out_specs=whole(half),
        compiler_params=params(4),
        name="add_cores",
    )(*near_core(mine, to_core(other)))
    landed = [home(x, t) for t, x in enumerate(sums)]
    moved = back(own)
    keep, send = pl.pallas_call(
        functools.partial(add_chips, stays),
        out_shape=[VMEM((r, d), f32)] * 2,
        in_specs=whole(1 + half),
        out_specs=whole(2),
        compiler_params=params(4),
        name="add_chips",
    )(*near_core(sums[-1], *landed))
    return pl.pallas_call(
        functools.partial(finish, stays),
        out_shape=jax.ShapeDtypeStruct((1, r, d), bf16),
        in_specs=whole(4),
        out_specs=pl.BlockSpec(memory_space=VMEM),
        scratch_shapes=[VMEM((1, d), f32)],
        compiler_params=params(4),
        name="finish",
    )(*near_core(own, moved, keep, to_core(send)))


def solution(mesh):
    return jax.shard_map(
        functools.partial(on_device, mesh.shape["section"], mesh.shape["seqtp"]),
        mesh=mesh,
        in_specs=(
            P("section", None, "seqtp", None),
            P("section", "seqtp", None),
            P("section"),
            P("section", None),
            P(None, "seqtp"),
            P(None, "seqtp"),
            P("seqtp", None),
        ),
        out_specs=P("section", "seqtp", None),
        check_vma=False,
    )
```

```python
import functools

import jax
import jax.numpy as jnp
from jax import lax
from jax.experimental import pallas as pl
from jax.experimental.pallas import tpu as pltpu
from jax.sharding import PartitionSpec as P

EPS = 1e-05
CORES = 2
VMEM = pltpu.VMEM


def whole(n):
    return [pl.BlockSpec(memory_space=VMEM)] * n


def anywhere(n):
    return [pl.BlockSpec(memory_space=pl.ANY)] * n


def near_core(*arrays):
    return [pltpu.with_memory_space_constraint(x, VMEM) for x in arrays]


def far_off(*arrays):
    return [pltpu.with_memory_space_constraint(x, pltpu.HBM) for x in arrays]


def params(mib):
    return pltpu.CompilerParams(vmem_limit_bytes=mib * 2**20)


def cost(bytes_accessed):
    return pl.CostEstimate(flops=0, bytes_accessed=bytes_accessed, transcendentals=0)


def on_chip_with(bit):
    return lax.rem(lax.div(lax.axis_index("seqtp"), CORES * max(bit, 1)), 2) == 1


def crossed(blocks, swap):
    out = list(blocks)
    for n in range(0, len(blocks) - 1, 2):
        a, b = blocks[n : n + 2]
        out[n], out[n + 1] = jnp.where(swap, a, b), jnp.where(swap, b, a)
    return out


def on_first_core():
    return lax.rem(lax.axis_index("seqtp"), CORES) == 0


def nn(left, weight):
    return jnp.dot(left, weight, preferred_element_type=jnp.float32)


def prepare(saved_hbm, grad_hbm, gain_hbm, saved_ref, grad_ref, gain_ref, sems):
    copies = [
        pltpu.make_async_copy(src, dst, sems.at[n])
        for n, (src, dst) in enumerate(((saved_hbm, saved_ref), (grad_hbm, grad_ref), (gain_hbm, gain_ref)))
    ]
    for copy in copies:
        copy.start()
    for copy in copies:
        copy.wait()


def join(slot_ref, saved_ref, other_saved_ref, grad_ref, other_grad_ref, gain_ref, rows_ref):
    r, d = grad_ref.shape[1:]
    first = on_first_core()
    slot = slot_ref[0]
    pairs = ((saved_ref[0, slot], other_saved_ref[0, slot]), (grad_ref[0], other_grad_ref[0]))
    for at, (mine, other) in enumerate(pairs):
        rows_ref[:r, at * d : (at + 1) * d] = jnp.where(first, mine, other)
        rows_ref[r:, at * d : (at + 1) * d] = jnp.where(first, other, mine)
    piece = rows_ref.shape[1] - 2 * d
    for n in range(rows_ref.shape[0]):
        rows_ref[n : n + 1, 2 * d :] = gain_ref[:, n * piece : (n + 1) * piece]


def fetch(gate_hbm, up_hbm, down_hbm, both_ref, gate_ref, up_ref, down_ref, sems, last_sem):
    d, h = gate_hbm.shape
    parts = sems.shape[1]
    rows = d // parts
    columns = (gate_hbm, up_hbm)
    copies = [
        [
            pltpu.make_async_copy(
                src.at[pl.ds(n * rows, rows)], both_ref.at[pl.ds(n * rows, rows), pl.ds(k * h, h)], sems.at[k, n]
            )
            for n in range(parts)
        ]
        for k, src in enumerate(columns)
    ]
    last = pltpu.make_async_copy(down_hbm, down_ref, last_sem)
    for copy in copies[0] + copies[1] + [last]:
        copy.start()
    for k, turned_ref in enumerate((gate_ref, up_ref)):
        for n, copy in enumerate(copies[k]):
            copy.wait()
            here = slice(n * rows, (n + 1) * rows)
            turned_ref[:, here] = both_ref[here, k * h : (k + 1) * h].T
    last.wait()


def turn(down_ref, after, turned_ref):
    d = turned_ref.shape[0]
    step = d // 8
    for n in range(0, d, step):
        turned_ref[n : n + step] = down_ref[:, n : n + step].T


def collect(turns, *refs):
    *blocks, after, out_ref, gain_ref = refs
    r = blocks[0].shape[0]
    first, turned = on_first_core(), on_chip_with(turns)
    came = [ref[:, : out_ref.shape[1]] for ref in blocks[::-1]]
    nearer = came[-1:] + came[:-1]
    farther = crossed(came, turned) if turns else came
    for n, (a, b) in enumerate(zip(nearer, farther)):
        out_ref[n * r : (n + 1) * r] = jnp.where(first, a, b)
    width = out_ref.shape[1]
    piece = blocks[0].shape[1] - width
    for n in range(r):
        gain_ref[:, n * piece : (n + 1) * piece] = blocks[0][n : n + 1, width:].astype(jnp.float32)


def arrange(near_ref, far_ref, gain_ref, normed_ref, grad_ref, own_ref, rows_ref):
    d = normed_ref.shape[1]
    half, r = near_ref.shape[0], own_ref.shape[0]
    first = on_first_core()
    near, far = near_ref[...].astype(jnp.float32), far_ref[...].astype(jnp.float32)
    rows_ref[:half] = jnp.where(first, near, far)
    rows_ref[half:] = jnp.where(first, far, near)
    grad_ref[...] = rows_ref[:, d:].astype(jnp.bfloat16)
    wide = rows_ref[:, :d]
    recip = lax.rsqrt(jnp.mean(wide * wide, axis=-1, keepdims=True) + EPS)
    normed_ref[...] = (wide * recip * gain_ref[...]).astype(jnp.bfloat16)
    own_ref[:, : 2 * d] = jnp.where(first, rows_ref[:r], rows_ref[r : 2 * r]).astype(jnp.bfloat16)
    piece = d // r
    for n in range(r):
        own_ref[n : n + 1, 2 * d :] = gain_ref[:, n * piece : (n + 1) * piece].astype(jnp.bfloat16)


def expert(rows, normed_ref, grad_ref, both_ref, gate_ref, up_ref, down_ref, mine_ref, other_ref):
    h = down_ref.shape[1]
    both = nn(normed_ref[...], both_ref[...])
    gate, up = both[:, :h], both[:, h:]
    d_hidden = nn(grad_ref[...], down_ref[...])
    p = jax.nn.sigmoid(gate)
    d_gate = d_hidden * up * p * (1.0 + gate * (1.0 - p))
    d_up = d_hidden * gate * p
    d_both = jnp.concatenate([d_gate, d_up], axis=1).astype(jnp.bfloat16)
    total = nn(d_both[:, :h], gate_ref[...]) + nn(d_both[:, h:], up_ref[...])
    first = on_first_core()
    for n in range(mine_ref.shape[0] // rows):
        even = total[2 * n * rows : (2 * n + 1) * rows]
        odd = total[(2 * n + 1) * rows : (2 * n + 2) * rows]
        mine_ref[n * rows : (n + 1) * rows] = jnp.where(first, even, odd)
        other_ref[n * rows : (n + 1) * rows] = jnp.where(first, odd, even)


def add_cores(turns, mine_ref, got_ref, *out_refs):
    total = (mine_ref[...] + got_ref[...]).astype(jnp.bfloat16)
    r = out_refs[0].shape[0]
    parts = [total[k * r : (k + 1) * r] for k in range(len(out_refs))]
    first = on_first_core()
    odd = crossed(parts, jnp.logical_not(on_chip_with(turns))) if turns else parts
    for ref, a, b in zip(out_refs, parts[::-1], odd):
        ref[...] = jnp.where(first, a, b)


def add_chips(stays, local_ref, *refs):
    *parts, keep_ref, send_ref = refs
    first = on_first_core()
    stayed = jnp.logical_and(first, stays(lax.axis_index("section")))
    total = jnp.where(stayed, local_ref[...], parts[-1][...]).astype(jnp.float32)
    for ref in parts[:-1]:
        total = total + ref[...].astype(jnp.float32)
    r = keep_ref.shape[0]
    keep_ref[...] = jnp.where(first, total[:r], total[r:])
    send_ref[...] = jnp.where(first, total[r:], total[:r])


def finish(stays, stayed_ref, moved_ref, keep_ref, got_ref, out_ref, gain_ref):
    r, d = keep_ref.shape
    here = stays(lax.axis_index("section"))
    own = jnp.where(here, stayed_ref[...].astype(jnp.float32), moved_ref[...].astype(jnp.float32))
    piece = d // r
    for n in range(r):
        gain_ref[:, n * piece : (n + 1) * piece] = own[n : n + 1, 2 * d :]
    wide, grad = own[:, :d], own[:, d : 2 * d]
    recip = lax.rsqrt(jnp.mean(wide * wide, axis=-1, keepdims=True) + EPS)
    scaled = gain_ref[...] * (keep_ref[...] + got_ref[...])
    unit = wide * recip
    mean = jnp.mean(scaled * unit, axis=-1, keepdims=True)
    out_ref[0] = (grad + recip * (scaled - unit * mean)).astype(out_ref.dtype)


def on_device(sections, members, saved_in, grad_in, slot_table, gain, w_gate, w_up, w_down):
    chips = members // CORES
    r, d = grad_in.shape[1:]
    hidden = w_down.shape[0]
    f32, bf16 = jnp.float32, jnp.bfloat16
    half = chips // CORES
    power = chips & (chips - 1) == 0
    out_turns, home_turns = (half, 1) if power else (0, 0)

    def swapped(n, t, bit, chip):
        return t ^ 1 if bit and chip & bit and t | 1 < n else t

    def route(goal):
        pairs = []
        for s in range(sections):
            for i in range(members):
                to, chip, *core = goal(s, *divmod(i, CORES))
                core = core[0] if core else i % CORES
                pairs.append((s * members + i, to % sections * members + chip % chips * CORES + core))
        return pairs

    even = sections % 2 == 0

    def beside(s):
        return s ^ 1 if even else s - 1

    def before(s):
        return s - 2 * (s % 2) if even else s

    def stays(section):
        return lax.rem(section, 2) == 0 if even else section >= 0

    def ahead(x, t):
        def goal(s, chip, core):
            k = half + swapped(half, t, out_turns, chip) if core else (t + 1) % half
            return beside(s), chip ^ k if power else chip + k

        return lax.ppermute(x, ("section", "seqtp"), route(goal))

    def home(x, t):
        def goal(s, chip, core):
            k = 2 * swapped(half, t, home_turns, chip) + 1 if core else 2 * (half - 1 - t)
            to = before(s) if k else s - 2 if even else s - 1
            return to, chip ^ k if power else chip - k

        return lax.ppermute(x, ("section", "seqtp"), route(goal))

    def back(x):
        return lax.ppermute(x, ("section", "seqtp"), route(lambda s, chip, core: (s, chip, core ^ 1) if before(s) == s else (before(s), chip)))

    def to_core(x):
        return lax.ppermute(x, "seqtp", [(i, i ^ 1) for i in range(members)])

    saved, grads, gain_row = pl.pallas_call(
        prepare,
        out_shape=[VMEM(saved_in.shape, bf16), VMEM(grad_in.shape, bf16), VMEM(gain.shape, bf16)],
        in_specs=anywhere(3),
        out_specs=whole(3),
        scratch_shapes=[pltpu.SemaphoreType.DMA((3,))],
        compiler_params=params(4),
        name="prepare",
    )(*far_off(saved_in, grad_in, gain))
    chip_rows = pl.pallas_call(
        join,
        out_shape=VMEM((CORES * r, 2 * d + d // (CORES * r)), bf16),
        in_specs=[pl.BlockSpec(memory_space=pltpu.SMEM)] + whole(5),
        out_specs=pl.BlockSpec(memory_space=VMEM),
        compiler_params=params(4),
        name="join",
    )(slot_table, *near_core(saved, to_core(saved_in), grads, to_core(grad_in), gain_row))
    both, gate_turned, up_turned, down = pl.pallas_call(
        fetch,
        out_shape=[VMEM((d, 2 * hidden), bf16)] + [VMEM((hidden, d), bf16)] * 3,
        in_specs=anywhere(3),
        out_specs=whole(4),
        scratch_shapes=[pltpu.SemaphoreType.DMA((2, 4)), pltpu.SemaphoreType.DMA],
        compiler_params=params(4),
        cost_estimate=cost(12 * d * hidden),
        name="fetch",
    )(*far_off(w_gate, w_up, w_down))
    blocks = [ahead(chip_rows, t) for t in range(half)]
    rows = chips * r
    block, gain_wide = pl.pallas_call(
        functools.partial(collect, out_turns),
        out_shape=[VMEM((rows, 2 * d), bf16), VMEM((1, d), f32)],
        in_specs=whole(len(blocks)) + anywhere(1),
        out_specs=whole(2),
        compiler_params=params(4),
        name="collect",
    )(*near_core(*blocks[::-1], both))
    far = to_core(block)
    down_turned = pl.pallas_call(
        turn,
        out_shape=VMEM((d, hidden), bf16),
        in_specs=whole(1) + anywhere(1),
        out_specs=pl.BlockSpec(memory_space=VMEM),
        compiler_params=params(4),
        cost_estimate=cost(4 * d * hidden),
        name="turn",
    )(*near_core(down, block))
    normed, grad, own = pl.pallas_call(
        arrange,
        out_shape=[VMEM((2 * rows, d), bf16)] * 2 + [VMEM((r, 2 * d + d // r), bf16)],
        in_specs=whole(3),
        out_specs=whole(3),
        scratch_shapes=[VMEM((2 * rows, 2 * d), f32)],
        compiler_params=params(16),
        name="arrange",
    )(*near_core(block, far, gain_wide))
    mine, other = pl.pallas_call(
        functools.partial(expert, CORES * r),
        out_shape=[VMEM((rows, d), f32)] * 2,
        in_specs=whole(6),
        out_specs=whole(2),
        compiler_params=params(16),
        name="expert",
    )(*near_core(normed, grad, both, gate_turned, up_turned, down_turned))
    sums = pl.pallas_call(
        functools.partial(add_cores, home_turns),
        out_shape=[VMEM((CORES * r, d), bf16)] * half,
        in_specs=whole(2),
        out_specs=whole(half),
        compiler_params=params(4),
        name="add_cores",
    )(*near_core(mine, to_core(other)))
    landed = [home(x, t) for t, x in enumerate(sums)]
    moved = back(own)
    keep, send = pl.pallas_call(
        functools.partial(add_chips, stays),
        out_shape=[VMEM((r, d), f32)] * 2,
        in_specs=whole(1 + half),
        out_specs=whole(2),
        compiler_params=params(4),
        name="add_chips",
    )(*near_core(sums[-1], *landed))
    return pl.pallas_call(
        functools.partial(finish, stays),
        out_shape=jax.ShapeDtypeStruct((1, r, d), bf16),
        in_specs=whole(4),
        out_specs=pl.BlockSpec(memory_space=VMEM),
        scratch_shapes=[VMEM((1, d), f32)],
        compiler_params=params(4),
        name="finish",
    )(*near_core(own, moved, keep, to_core(send)))


def solution(mesh):
    return jax.shard_map(
        functools.partial(on_device, mesh.shape["section"], mesh.shape["seqtp"]),
        mesh=mesh,
        in_specs=(
            P("section", None, "seqtp", None),
            P("section", "seqtp", None),
            P("section"),
            P("section", None),
            P(None, "seqtp"),
            P(None, "seqtp"),
            P("seqtp", None),
        ),
        out_specs=P("section", "seqtp", None),
        check_vma=False,
    )
```

```python
import functools

import jax
import jax.numpy as jnp
from jax import lax
from jax.experimental import pallas as pl
from jax.experimental.pallas import tpu as pltpu
from jax.sharding import PartitionSpec as P

EPS = 1e-05
CORES = 2
VMEM = pltpu.VMEM


def whole(n):
    return [pl.BlockSpec(memory_space=VMEM)] * n


def anywhere(n):
    return [pl.BlockSpec(memory_space=pl.ANY)] * n


def near_core(*arrays):
    return [pltpu.with_memory_space_constraint(x, VMEM) for x in arrays]


def far_off(*arrays):
    return [pltpu.with_memory_space_constraint(x, pltpu.HBM) for x in arrays]


def params(mib):
    return pltpu.CompilerParams(vmem_limit_bytes=mib * 2**20)


def cost(bytes_accessed):
    return pl.CostEstimate(flops=0, bytes_accessed=bytes_accessed, transcendentals=0)


def on_chip_with(bit):
    return lax.rem(lax.div(lax.axis_index("seqtp"), CORES * max(bit, 1)), 2) == 1


def crossed(blocks, swap):
    out = list(blocks)
    for n in range(0, len(blocks) - 1, 2):
        a, b = blocks[n : n + 2]
        out[n], out[n + 1] = jnp.where(swap, a, b), jnp.where(swap, b, a)
    return out


def on_first_core():
    return lax.rem(lax.axis_index("seqtp"), CORES) == 0


def nn(left, weight):
    return jnp.dot(left, weight, preferred_element_type=jnp.float32)


def prepare(slot_ref, saved_hbm, grad_hbm, gain_hbm, mine_ref, gain_ref, sems):
    d = grad_hbm.shape[-1]
    copies = [
        pltpu.make_async_copy(src, dst, sems.at[n])
        for n, (src, dst) in enumerate(
            (
                (saved_hbm.at[0, slot_ref[0]], mine_ref.at[:, pl.ds(0, d)]),
                (grad_hbm.at[0], mine_ref.at[:, pl.ds(d, d)]),
                (gain_hbm, gain_ref),
            )
        )
    ]
    for copy in copies:
        copy.start()
    for copy in copies:
        copy.wait()


def join(slot_ref, mine_ref, saved_ref, grad_ref, gain_ref, rows_ref):
    r, d = grad_ref.shape[1:]
    first = on_first_core()
    for at, other in enumerate((saved_ref[0, slot_ref[0]], grad_ref[0])):
        part = slice(at * d, (at + 1) * d)
        mine = mine_ref[:, part]
        rows_ref[:r, part] = jnp.where(first, mine, other)
        rows_ref[r:, part] = jnp.where(first, other, mine)
    piece = rows_ref.shape[1] - 2 * d
    for n in range(rows_ref.shape[0]):
        rows_ref[n : n + 1, 2 * d :] = gain_ref[:, n * piece : (n + 1) * piece]


def fetch(gate_hbm, up_hbm, down_hbm, both_ref, gate_ref, up_ref, down_ref, sems, last_sem):
    d, h = gate_hbm.shape
    parts = sems.shape[1]
    rows = d // parts
    columns = (gate_hbm, up_hbm)
    copies = [
        [
            pltpu.make_async_copy(
                src.at[pl.ds(n * rows, rows)], both_ref.at[pl.ds(n * rows, rows), pl.ds(k * h, h)], sems.at[k, n]
            )
            for n in range(parts)
        ]
        for k, src in enumerate(columns)
    ]
    last = pltpu.make_async_copy(down_hbm, down_ref, last_sem)
    for copy in copies[0] + copies[1] + [last]:
        copy.start()
    for k, turned_ref in enumerate((gate_ref, up_ref)):
        for n, copy in enumerate(copies[k]):
            copy.wait()
            here = slice(n * rows, (n + 1) * rows)
            turned_ref[:, here] = both_ref[here, k * h : (k + 1) * h].T
    last.wait()


def turn(down_ref, after, turned_ref):
    d = turned_ref.shape[0]
    step = d // 8
    for n in range(0, d, step):
        turned_ref[n : n + step] = down_ref[:, n : n + step].T


def collect(turns, *refs):
    *blocks, after, out_ref, gain_ref = refs
    r = blocks[0].shape[0]
    first, turned = on_first_core(), on_chip_with(turns)
    came = [ref[:, : out_ref.shape[1]] for ref in blocks[::-1]]
    nearer = came[-1:] + came[:-1]
    farther = crossed(came, turned) if turns else came
    for n, (a, b) in enumerate(zip(nearer, farther)):
        out_ref[n * r : (n + 1) * r] = jnp.where(first, a, b)
    width = out_ref.shape[1]
    piece = blocks[0].shape[1] - width
    for n in range(r):
        gain_ref[:, n * piece : (n + 1) * piece] = blocks[0][n : n + 1, width:].astype(jnp.float32)


def arrange(near_ref, far_ref, gain_ref, normed_ref, grad_ref, own_ref, rows_ref):
    d = normed_ref.shape[1]
    half, r = near_ref.shape[0], own_ref.shape[0]
    first = on_first_core()
    near, far = near_ref[...].astype(jnp.float32), far_ref[...].astype(jnp.float32)
    rows_ref[:half] = jnp.where(first, near, far)
    rows_ref[half:] = jnp.where(first, far, near)
    grad_ref[...] = rows_ref[:, d:].astype(jnp.bfloat16)
    wide = rows_ref[:, :d]
    recip = lax.rsqrt(jnp.mean(wide * wide, axis=-1, keepdims=True) + EPS)
    normed_ref[...] = (wide * recip * gain_ref[...]).astype(jnp.bfloat16)
    own_ref[:, : 2 * d] = jnp.where(first, rows_ref[:r], rows_ref[r : 2 * r]).astype(jnp.bfloat16)
    piece = d // r
    for n in range(r):
        own_ref[n : n + 1, 2 * d :] = gain_ref[:, n * piece : (n + 1) * piece].astype(jnp.bfloat16)


def expert(rows, normed_ref, grad_ref, both_ref, gate_ref, up_ref, down_ref, mine_ref, other_ref):
    h = down_ref.shape[1]
    both = nn(normed_ref[...], both_ref[...])
    gate, up = both[:, :h], both[:, h:]
    d_hidden = nn(grad_ref[...], down_ref[...])
    p = jax.nn.sigmoid(gate)
    d_gate = d_hidden * up * p * (1.0 + gate * (1.0 - p))
    d_up = d_hidden * gate * p
    d_both = jnp.concatenate([d_gate, d_up], axis=1).astype(jnp.bfloat16)
    total = nn(d_both[:, :h], gate_ref[...]) + nn(d_both[:, h:], up_ref[...])
    first = on_first_core()
    for n in range(mine_ref.shape[0] // rows):
        even = total[2 * n * rows : (2 * n + 1) * rows]
        odd = total[(2 * n + 1) * rows : (2 * n + 2) * rows]
        mine_ref[n * rows : (n + 1) * rows] = jnp.where(first, even, odd)
        other_ref[n * rows : (n + 1) * rows] = jnp.where(first, odd, even)


def add_cores(turns, mine_ref, got_ref, *out_refs):
    total = (mine_ref[...] + got_ref[...]).astype(jnp.bfloat16)
    r = out_refs[0].shape[0]
    parts = [total[k * r : (k + 1) * r] for k in range(len(out_refs))]
    first = on_first_core()
    odd = crossed(parts, jnp.logical_not(on_chip_with(turns))) if turns else parts
    for ref, a, b in zip(out_refs, parts[::-1], odd):
        ref[...] = jnp.where(first, a, b)


def add_chips(stays, local_ref, *refs):
    *parts, keep_ref, send_ref = refs
    first = on_first_core()
    stayed = jnp.logical_and(first, stays(lax.axis_index("section")))
    total = jnp.where(stayed, local_ref[...], parts[-1][...]).astype(jnp.float32)
    for ref in parts[:-1]:
        total = total + ref[...].astype(jnp.float32)
    r = keep_ref.shape[0]
    keep_ref[...] = jnp.where(first, total[:r], total[r:])
    send_ref[...] = jnp.where(first, total[r:], total[:r])


def settle(stays, stayed_ref, moved_ref, keep_ref, unit_ref, gain_ref, kept_ref, base_ref, recip_ref):
    r, d = keep_ref.shape
    here = stays(lax.axis_index("section"))
    own = jnp.where(here, stayed_ref[...].astype(jnp.float32), moved_ref[...].astype(jnp.float32))
    piece = d // r
    for n in range(r):
        gain_ref[:, n * piece : (n + 1) * piece] = own[n : n + 1, 2 * d :]
    wide = own[:, :d]
    recip = lax.rsqrt(jnp.mean(wide * wide, axis=-1, keepdims=True) + EPS)
    unit_ref[...] = wide * recip
    kept_ref[...] = gain_ref[...] * keep_ref[...]
    base_ref[...] = own[:, d : 2 * d]
    recip_ref[...] = jnp.broadcast_to(recip, recip_ref.shape)


def finish(unit_ref, gain_ref, kept_ref, base_ref, recip_ref, got_ref, out_ref):
    unit, recip = unit_ref[...], recip_ref[:, :1]
    scaled = kept_ref[...] + gain_ref[...] * got_ref[...]
    mean = jnp.mean(scaled * unit, axis=-1, keepdims=True)
    out_ref[0] = (base_ref[...] + recip * (scaled - unit * mean)).astype(out_ref.dtype)


def on_device(sections, members, saved_in, grad_in, slot_table, gain, w_gate, w_up, w_down):
    chips = members // CORES
    r, d = grad_in.shape[1:]
    hidden = w_down.shape[0]
    f32, bf16 = jnp.float32, jnp.bfloat16
    half = chips // CORES
    power = chips & (chips - 1) == 0
    out_turns, home_turns = (half, 1) if power else (0, 0)

    def swapped(n, t, bit, chip):
        return t ^ 1 if bit and chip & bit and t | 1 < n else t

    def route(goal):
        pairs = []
        for s in range(sections):
            for i in range(members):
                to, chip, *core = goal(s, *divmod(i, CORES))
                core = core[0] if core else i % CORES
                pairs.append((s * members + i, to % sections * members + chip % chips * CORES + core))
        return pairs

    even = sections % 2 == 0

    def beside(s):
        return s ^ 1 if even else s - 1

    def before(s):
        return s - 2 * (s % 2) if even else s

    def stays(section):
        return lax.rem(section, 2) == 0 if even else section >= 0

    def ahead(x, t):
        def goal(s, chip, core):
            k = half + swapped(half, t, out_turns, chip) if core else (t + 1) % half
            return beside(s), chip ^ k if power else chip + k

        return lax.ppermute(x, ("section", "seqtp"), route(goal))

    def home(x, t):
        def goal(s, chip, core):
            k = 2 * swapped(half, t, home_turns, chip) + 1 if core else 2 * (half - 1 - t)
            to = before(s) if k else s - 2 if even else s - 1
            return to, chip ^ k if power else chip - k

        return lax.ppermute(x, ("section", "seqtp"), route(goal))

    def back(x):
        return lax.ppermute(x, ("section", "seqtp"), route(lambda s, chip, core: (s, chip, core ^ 1) if before(s) == s else (before(s), chip)))

    def to_core(x):
        return lax.ppermute(x, "seqtp", [(i, i ^ 1) for i in range(members)])

    scalar = pl.BlockSpec(memory_space=pltpu.SMEM)
    mine, gain_row = pl.pallas_call(
        prepare,
        out_shape=[VMEM((r, 2 * d), bf16), VMEM(gain.shape, bf16)],
        in_specs=[scalar] + anywhere(3),
        out_specs=whole(2),
        scratch_shapes=[pltpu.SemaphoreType.DMA((3,))],
        compiler_params=params(4),
        name="prepare",
    )(slot_table, *far_off(saved_in, grad_in, gain))
    chip_rows = pl.pallas_call(
        join,
        out_shape=VMEM((CORES * r, 2 * d + d // (CORES * r)), bf16),
        in_specs=[scalar] + whole(4),
        out_specs=pl.BlockSpec(memory_space=VMEM),
        compiler_params=params(4),
        name="join",
    )(slot_table, *near_core(mine, to_core(saved_in), to_core(grad_in), gain_row))
    both, gate_turned, up_turned, down = pl.pallas_call(
        fetch,
        out_shape=[VMEM((d, 2 * hidden), bf16)] + [VMEM((hidden, d), bf16)] * 3,
        in_specs=anywhere(3),
        out_specs=whole(4),
        scratch_shapes=[pltpu.SemaphoreType.DMA((2, 4)), pltpu.SemaphoreType.DMA],
        compiler_params=params(4),
        cost_estimate=cost(12 * d * hidden),
        name="fetch",
    )(*far_off(w_gate, w_up, w_down))
    blocks = [ahead(chip_rows, t) for t in range(half)]
    rows = chips * r
    block, gain_wide = pl.pallas_call(
        functools.partial(collect, out_turns),
        out_shape=[VMEM((rows, 2 * d), bf16), VMEM((1, d), f32)],
        in_specs=whole(len(blocks)) + anywhere(1),
        out_specs=whole(2),
        compiler_params=params(4),
        name="collect",
    )(*near_core(*blocks[::-1], both))
    far = to_core(block)
    down_turned = pl.pallas_call(
        turn,
        out_shape=VMEM((d, hidden), bf16),
        in_specs=whole(1) + anywhere(1),
        out_specs=pl.BlockSpec(memory_space=VMEM),
        compiler_params=params(4),
        cost_estimate=cost(4 * d * hidden),
        name="turn",
    )(*near_core(down, block))
    normed, grad, own = pl.pallas_call(
        arrange,
        out_shape=[VMEM((2 * rows, d), bf16)] * 2 + [VMEM((r, 2 * d + d // r), bf16)],
        in_specs=whole(3),
        out_specs=whole(3),
        scratch_shapes=[VMEM((2 * rows, 2 * d), f32)],
        compiler_params=params(16),
        name="arrange",
    )(*near_core(block, far, gain_wide))
    mine, other = pl.pallas_call(
        functools.partial(expert, CORES * r),
        out_shape=[VMEM((rows, d), f32)] * 2,
        in_specs=whole(6),
        out_specs=whole(2),
        compiler_params=params(16),
        name="expert",
    )(*near_core(normed, grad, both, gate_turned, up_turned, down_turned))
    sums = pl.pallas_call(
        functools.partial(add_cores, home_turns),
        out_shape=[VMEM((CORES * r, d), bf16)] * half,
        in_specs=whole(2),
        out_specs=whole(half),
        compiler_params=params(4),
        name="add_cores",
    )(*near_core(mine, to_core(other)))
    landed = [home(x, t) for t, x in enumerate(sums)]
    moved = back(own)
    keep, send = pl.pallas_call(
        functools.partial(add_chips, stays),
        out_shape=[VMEM((r, d), f32)] * 2,
        in_specs=whole(1 + half),
        out_specs=whole(2),
        compiler_params=params(4),
        name="add_chips",
    )(*near_core(sums[-1], *landed))
    settled = pl.pallas_call(
        functools.partial(settle, stays),
        out_shape=[VMEM(dims, f32) for dims in ((r, d), (1, d), (r, d), (r, d), (r, 128))],
        in_specs=whole(3),
        out_specs=whole(5),
        compiler_params=params(4),
        name="settle",
    )(*near_core(own, moved, keep))
    return pl.pallas_call(
        finish,
        out_shape=jax.ShapeDtypeStruct((1, r, d), bf16),
        in_specs=whole(6),
        out_specs=pl.BlockSpec(memory_space=VMEM),
        compiler_params=params(4),
        name="finish",
    )(*near_core(*settled, to_core(send)))


def solution(mesh):
    return jax.shard_map(
        functools.partial(on_device, mesh.shape["section"], mesh.shape["seqtp"]),
        mesh=mesh,
        in_specs=(
            P("section", None, "seqtp", None),
            P("section", "seqtp", None),
            P("section"),
            P("section", None),
            P(None, "seqtp"),
            P(None, "seqtp"),
            P("seqtp", None),
        ),
        out_specs=P("section", "seqtp", None),
        check_vma=False,
    )
```

```python
import functools

import jax
import jax.numpy as jnp
from jax import lax
from jax.experimental import pallas as pl
from jax.experimental.pallas import tpu as pltpu
from jax.sharding import PartitionSpec as P

EPS = 1e-05
CORES = 2
VMEM = pltpu.VMEM


def whole(n):
    return [pl.BlockSpec(memory_space=VMEM)] * n


def anywhere(n):
    return [pl.BlockSpec(memory_space=pl.ANY)] * n


def near_core(*arrays):
    return [pltpu.with_memory_space_constraint(x, VMEM) for x in arrays]


def far_off(*arrays):
    return [pltpu.with_memory_space_constraint(x, pltpu.HBM) for x in arrays]


def params(mib):
    return pltpu.CompilerParams(vmem_limit_bytes=mib * 2**20)


def cost(bytes_accessed):
    return pl.CostEstimate(flops=0, bytes_accessed=bytes_accessed, transcendentals=0)


def on_chip_with(bit):
    return lax.rem(lax.div(lax.axis_index("seqtp"), CORES * max(bit, 1)), 2) == 1


def crossed(blocks, swap):
    out = list(blocks)
    for n in range(0, len(blocks) - 1, 2):
        a, b = blocks[n : n + 2]
        out[n], out[n + 1] = jnp.where(swap, a, b), jnp.where(swap, b, a)
    return out


def on_first_core():
    return lax.rem(lax.axis_index("seqtp"), CORES) == 0


def nn(left, weight):
    return jnp.dot(left, weight, preferred_element_type=jnp.float32)


def prepare(slot_ref, saved_hbm, grad_hbm, gain_hbm, mine_ref, gain_ref, sems):
    d = grad_hbm.shape[-1]
    copies = [
        pltpu.make_async_copy(src, dst, sems.at[n])
        for n, (src, dst) in enumerate(
            (
                (saved_hbm.at[0, slot_ref[0]], mine_ref.at[:, pl.ds(0, d)]),
                (grad_hbm.at[0], mine_ref.at[:, pl.ds(d, d)]),
                (gain_hbm, gain_ref),
            )
        )
    ]
    for copy in copies:
        copy.start()
    for copy in copies:
        copy.wait()


def join(slot_ref, mine_ref, saved_ref, grad_ref, gain_ref, rows_ref):
    r, d = grad_ref.shape[1:]
    first = on_first_core()
    for at, other in enumerate((saved_ref[0, slot_ref[0]], grad_ref[0])):
        part = slice(at * d, (at + 1) * d)
        mine = mine_ref[:, part]
        rows_ref[:r, part] = jnp.where(first, mine, other)
        rows_ref[r:, part] = jnp.where(first, other, mine)
    piece = rows_ref.shape[1] - 2 * d
    for n in range(rows_ref.shape[0]):
        rows_ref[n : n + 1, 2 * d :] = gain_ref[:, n * piece : (n + 1) * piece]


def fetch(gate_hbm, up_hbm, down_hbm, both_ref, gate_ref, up_ref, down_ref, sems, last_sem):
    d, h = gate_hbm.shape
    parts = sems.shape[1]
    rows = d // parts
    columns = (gate_hbm, up_hbm)
    copies = [
        [
            pltpu.make_async_copy(
                src.at[pl.ds(n * rows, rows)], both_ref.at[pl.ds(n * rows, rows), pl.ds(k * h, h)], sems.at[k, n]
            )
            for n in range(parts)
        ]
        for k, src in enumerate(columns)
    ]
    last = pltpu.make_async_copy(down_hbm, down_ref, last_sem)
    for copy in copies[0] + copies[1] + [last]:
        copy.start()
    for k, turned_ref in enumerate((gate_ref, up_ref)):
        for n, copy in enumerate(copies[k]):
            copy.wait()
            here = slice(n * rows, (n + 1) * rows)
            turned_ref[:, here] = both_ref[here, k * h : (k + 1) * h].T
    last.wait()


def turn(down_ref, after, turned_ref):
    d = turned_ref.shape[0]
    step = d // 8
    for n in range(0, d, step):
        turned_ref[n : n + step] = down_ref[:, n : n + step].T


def collect(turns, *refs):
    *blocks, after, out_ref, gain_ref = refs
    r = blocks[0].shape[0]
    first, turned = on_first_core(), on_chip_with(turns)
    came = [ref[:, : out_ref.shape[1]] for ref in blocks[::-1]]
    nearer = came[-1:] + came[:-1]
    farther = crossed(came, turned) if turns else came
    for n, (a, b) in enumerate(zip(nearer, farther)):
        out_ref[n * r : (n + 1) * r] = jnp.where(first, a, b)
    width = out_ref.shape[1]
    piece = blocks[0].shape[1] - width
    for n in range(r):
        gain_ref[:, n * piece : (n + 1) * piece] = blocks[0][n : n + 1, width:].astype(jnp.float32)


def arrange(near_ref, far_ref, gain_ref, normed_ref, grad_ref, own_ref, rows_ref):
    d = normed_ref.shape[1]
    half, r = near_ref.shape[0], own_ref.shape[0]
    first = on_first_core()
    near, far = near_ref[...].astype(jnp.float32), far_ref[...].astype(jnp.float32)
    rows_ref[:half] = jnp.where(first, near, far)
    rows_ref[half:] = jnp.where(first, far, near)
    grad_ref[...] = rows_ref[:, d:].astype(jnp.bfloat16)
    wide = rows_ref[:, :d]
    recip = lax.rsqrt(jnp.mean(wide * wide, axis=-1, keepdims=True) + EPS)
    normed_ref[...] = (wide * recip * gain_ref[...]).astype(jnp.bfloat16)
    own_ref[:, : 2 * d] = jnp.where(first, rows_ref[:r], rows_ref[r : 2 * r]).astype(jnp.bfloat16)
    piece = d // r
    for n in range(r):
        own_ref[n : n + 1, 2 * d :] = gain_ref[:, n * piece : (n + 1) * piece].astype(jnp.bfloat16)


def expert(rows, normed_ref, grad_ref, both_ref, gate_ref, up_ref, down_ref, mine_ref, other_ref):
    h = down_ref.shape[1]
    both = nn(normed_ref[...], both_ref[...])
    gate, up = both[:, :h], both[:, h:]
    d_hidden = nn(grad_ref[...], down_ref[...])
    p = jax.nn.sigmoid(gate)
    d_gate = d_hidden * up * p * (1.0 + gate * (1.0 - p))
    d_up = d_hidden * gate * p
    d_both = jnp.concatenate([d_gate, d_up], axis=1).astype(jnp.bfloat16)
    total = nn(d_both[:, :h], gate_ref[...]) + nn(d_both[:, h:], up_ref[...])
    first = on_first_core()
    for n in range(mine_ref.shape[0] // rows):
        even = total[2 * n * rows : (2 * n + 1) * rows]
        odd = total[(2 * n + 1) * rows : (2 * n + 2) * rows]
        mine_ref[n * rows : (n + 1) * rows] = jnp.where(first, even, odd)
        other_ref[n * rows : (n + 1) * rows] = jnp.where(first, odd, even).astype(other_ref.dtype)


def add_cores(turns, mine_ref, got_ref, *out_refs):
    total = (mine_ref[...] + got_ref[...].astype(jnp.float32)).astype(jnp.bfloat16)
    r = out_refs[0].shape[0]
    parts = [total[k * r : (k + 1) * r] for k in range(len(out_refs))]
    first = on_first_core()
    odd = crossed(parts, jnp.logical_not(on_chip_with(turns))) if turns else parts
    for ref, a, b in zip(out_refs, parts[::-1], odd):
        ref[...] = jnp.where(first, a, b)


def add_chips(stays, local_ref, *refs):
    *parts, keep_ref, send_ref = refs
    first = on_first_core()
    stayed = jnp.logical_and(first, stays(lax.axis_index("section")))
    total = jnp.where(stayed, local_ref[...], parts[-1][...]).astype(jnp.float32)
    for ref in parts[:-1]:
        total = total + ref[...].astype(jnp.float32)
    r = keep_ref.shape[0]
    keep_ref[...] = jnp.where(first, total[:r], total[r:])
    send_ref[...] = jnp.where(first, total[r:], total[:r])


def settle(stays, stayed_ref, moved_ref, keep_ref, unit_ref, gain_ref, kept_ref, base_ref, recip_ref):
    r, d = keep_ref.shape
    here = stays(lax.axis_index("section"))
    own = jnp.where(here, stayed_ref[...].astype(jnp.float32), moved_ref[...].astype(jnp.float32))
    piece = d // r
    for n in range(r):
        gain_ref[:, n * piece : (n + 1) * piece] = own[n : n + 1, 2 * d :]
    wide = own[:, :d]
    recip = lax.rsqrt(jnp.mean(wide * wide, axis=-1, keepdims=True) + EPS)
    unit_ref[...] = wide * recip
    kept_ref[...] = gain_ref[...] * keep_ref[...]
    base_ref[...] = own[:, d : 2 * d]
    recip_ref[...] = jnp.broadcast_to(recip, recip_ref.shape)


def finish(unit_ref, gain_ref, kept_ref, base_ref, recip_ref, got_ref, out_ref):
    unit, recip = unit_ref[...], recip_ref[:, :1]
    scaled = kept_ref[...] + gain_ref[...] * got_ref[...]
    mean = jnp.mean(scaled * unit, axis=-1, keepdims=True)
    out_ref[0] = (base_ref[...] + recip * (scaled - unit * mean)).astype(out_ref.dtype)


def on_device(sections, members, saved_in, grad_in, slot_table, gain, w_gate, w_up, w_down):
    chips = members // CORES
    r, d = grad_in.shape[1:]
    hidden = w_down.shape[0]
    f32, bf16 = jnp.float32, jnp.bfloat16
    half = chips // CORES
    power = chips & (chips - 1) == 0
    out_turns, home_turns = (half, 1) if power else (0, 0)

    def swapped(n, t, bit, chip):
        return t ^ 1 if bit and chip & bit and t | 1 < n else t

    def route(goal):
        pairs = []
        for s in range(sections):
            for i in range(members):
                to, chip, *core = goal(s, *divmod(i, CORES))
                core = core[0] if core else i % CORES
                pairs.append((s * members + i, to % sections * members + chip % chips * CORES + core))
        return pairs

    even = sections % 2 == 0

    def beside(s):
        return s ^ 1 if even else s - 1

    def before(s):
        return s - 2 * (s % 2) if even else s

    def stays(section):
        return lax.rem(section, 2) == 0 if even else section >= 0

    def ahead(x, t):
        def goal(s, chip, core):
            k = half + swapped(half, t, out_turns, chip) if core else (t + 1) % half
            return beside(s), chip ^ k if power else chip + k

        return lax.ppermute(x, ("section", "seqtp"), route(goal))

    def home(x, t):
        def goal(s, chip, core):
            k = 2 * swapped(half, t, home_turns, chip) + 1 if core else 2 * (half - 1 - t)
            to = before(s) if k else s - 2 if even else s - 1
            return to, chip ^ k if power else chip - k

        return lax.ppermute(x, ("section", "seqtp"), route(goal))

    def back(x):
        return lax.ppermute(x, ("section", "seqtp"), route(lambda s, chip, core: (s, chip, core ^ 1) if before(s) == s else (before(s), chip)))

    def to_core(x):
        return lax.ppermute(x, "seqtp", [(i, i ^ 1) for i in range(members)])

    scalar = pl.BlockSpec(memory_space=pltpu.SMEM)
    mine, gain_row = pl.pallas_call(
        prepare,
        out_shape=[VMEM((r, 2 * d), bf16), VMEM(gain.shape, bf16)],
        in_specs=[scalar] + anywhere(3),
        out_specs=whole(2),
        scratch_shapes=[pltpu.SemaphoreType.DMA((3,))],
        compiler_params=params(4),
        name="prepare",
    )(slot_table, *far_off(saved_in, grad_in, gain))
    chip_rows = pl.pallas_call(
        join,
        out_shape=VMEM((CORES * r, 2 * d + d // (CORES * r)), bf16),
        in_specs=[scalar] + whole(4),
        out_specs=pl.BlockSpec(memory_space=VMEM),
        compiler_params=params(4),
        name="join",
    )(slot_table, *near_core(mine, to_core(saved_in), to_core(grad_in), gain_row))
    both, gate_turned, up_turned, down = pl.pallas_call(
        fetch,
        out_shape=[VMEM((d, 2 * hidden), bf16)] + [VMEM((hidden, d), bf16)] * 3,
        in_specs=anywhere(3),
        out_specs=whole(4),
        scratch_shapes=[pltpu.SemaphoreType.DMA((2, 4)), pltpu.SemaphoreType.DMA],
        compiler_params=params(4),
        cost_estimate=cost(12 * d * hidden),
        name="fetch",
    )(*far_off(w_gate, w_up, w_down))
    blocks = [ahead(chip_rows, t) for t in range(half)]
    rows = chips * r
    block, gain_wide = pl.pallas_call(
        functools.partial(collect, out_turns),
        out_shape=[VMEM((rows, 2 * d), bf16), VMEM((1, d), f32)],
        in_specs=whole(len(blocks)) + anywhere(1),
        out_specs=whole(2),
        compiler_params=params(4),
        name="collect",
    )(*near_core(*blocks[::-1], both))
    far = to_core(block)
    down_turned = pl.pallas_call(
        turn,
        out_shape=VMEM((d, hidden), bf16),
        in_specs=whole(1) + anywhere(1),
        out_specs=pl.BlockSpec(memory_space=VMEM),
        compiler_params=params(4),
        cost_estimate=cost(4 * d * hidden),
        name="turn",
    )(*near_core(down, block))
    normed, grad, own = pl.pallas_call(
        arrange,
        out_shape=[VMEM((2 * rows, d), bf16)] * 2 + [VMEM((r, 2 * d + d // r), bf16)],
        in_specs=whole(3),
        out_specs=whole(3),
        scratch_shapes=[VMEM((2 * rows, 2 * d), f32)],
        compiler_params=params(16),
        name="arrange",
    )(*near_core(block, far, gain_wide))
    mine, other = pl.pallas_call(
        functools.partial(expert, CORES * r),
        out_shape=[VMEM((rows, d), f32), VMEM((rows, d), bf16)],
        in_specs=whole(6),
        out_specs=whole(2),
        compiler_params=params(16),
        name="expert",
    )(*near_core(normed, grad, both, gate_turned, up_turned, down_turned))
    sums = pl.pallas_call(
        functools.partial(add_cores, home_turns),
        out_shape=[VMEM((CORES * r, d), bf16)] * half,
        in_specs=whole(2),
        out_specs=whole(half),
        compiler_params=params(4),
        name="add_cores",
    )(*near_core(mine, to_core(other)))
    landed = [home(x, t) for t, x in enumerate(sums)]
    moved = back(own)
    keep, send = pl.pallas_call(
        functools.partial(add_chips, stays),
        out_shape=[VMEM((r, d), f32)] * 2,
        in_specs=whole(1 + half),
        out_specs=whole(2),
        compiler_params=params(4),
        name="add_chips",
    )(*near_core(sums[-1], *landed))
    settled = pl.pallas_call(
        functools.partial(settle, stays),
        out_shape=[VMEM(dims, f32) for dims in ((r, d), (1, d), (r, d), (r, d), (r, 128))],
        in_specs=whole(3),
        out_specs=whole(5),
        compiler_params=params(4),
        name="settle",
    )(*near_core(own, moved, keep))
    return pl.pallas_call(
        finish,
        out_shape=jax.ShapeDtypeStruct((1, r, d), bf16),
        in_specs=whole(6),
        out_specs=pl.BlockSpec(memory_space=VMEM),
        compiler_params=params(4),
        name="finish",
    )(*near_core(*settled, to_core(send)))


def solution(mesh):
    return jax.shard_map(
        functools.partial(on_device, mesh.shape["section"], mesh.shape["seqtp"]),
        mesh=mesh,
        in_specs=(
            P("section", None, "seqtp", None),
            P("section", "seqtp", None),
            P("section"),
            P("section", None),
            P(None, "seqtp"),
            P(None, "seqtp"),
            P("seqtp", None),
        ),
        out_specs=P("section", "seqtp", None),
        check_vma=False,
    )
```

```python
import functools

import jax
import jax.numpy as jnp
from jax import lax
from jax.experimental import pallas as pl
from jax.experimental.pallas import tpu as pltpu
from jax.sharding import PartitionSpec as P

EPS = 1e-05
CORES = 2
VMEM = pltpu.VMEM


def whole(n):
    return [pl.BlockSpec(memory_space=VMEM)] * n


def anywhere(n):
    return [pl.BlockSpec(memory_space=pl.ANY)] * n


def near_core(*arrays):
    return [pltpu.with_memory_space_constraint(x, VMEM) for x in arrays]


def far_off(*arrays):
    return [pltpu.with_memory_space_constraint(x, pltpu.HBM) for x in arrays]


def params(mib):
    return pltpu.CompilerParams(vmem_limit_bytes=mib * 2**20)


def cost(bytes_accessed):
    return pl.CostEstimate(flops=0, bytes_accessed=bytes_accessed, transcendentals=0)


def on_chip_with(bit):
    return lax.rem(lax.div(lax.axis_index("seqtp"), CORES * max(bit, 1)), 2) == 1


def crossed(blocks, swap):
    out = list(blocks)
    for n in range(0, len(blocks) - 1, 2):
        a, b = blocks[n : n + 2]
        out[n], out[n + 1] = jnp.where(swap, a, b), jnp.where(swap, b, a)
    return out


def on_first_core():
    return lax.rem(lax.axis_index("seqtp"), CORES) == 0


def nn(left, weight):
    return jnp.dot(left, weight, preferred_element_type=jnp.float32)


def prepare(slot_ref, saved_hbm, grad_hbm, gain_hbm, mine_ref, gain_ref, sems):
    d = grad_hbm.shape[-1]
    copies = [
        pltpu.make_async_copy(src, dst, sems.at[n])
        for n, (src, dst) in enumerate(
            (
                (saved_hbm.at[0, slot_ref[0]], mine_ref.at[:, pl.ds(0, d)]),
                (grad_hbm.at[0], mine_ref.at[:, pl.ds(d, d)]),
                (gain_hbm, gain_ref),
            )
        )
    ]
    for copy in copies:
        copy.start()
    for copy in copies:
        copy.wait()


def join(slot_ref, mine_ref, saved_ref, grad_ref, gain_ref, rows_ref):
    r, d = grad_ref.shape[1:]
    first = on_first_core()
    for at, other in enumerate((saved_ref[0, slot_ref[0]], grad_ref[0])):
        part = slice(at * d, (at + 1) * d)
        mine = mine_ref[:, part]
        rows_ref[:r, part] = jnp.where(first, mine, other)
        rows_ref[r:, part] = jnp.where(first, other, mine)
    piece = rows_ref.shape[1] - 2 * d
    for n in range(rows_ref.shape[0]):
        rows_ref[n : n + 1, 2 * d :] = gain_ref[:, n * piece : (n + 1) * piece]


def fetch(gate_hbm, up_hbm, down_hbm, both_ref, gate_ref, up_ref, down_ref, sems, last_sem):
    d, h = gate_hbm.shape
    parts = sems.shape[1]
    rows = d // parts
    columns = (gate_hbm, up_hbm)
    copies = [
        [
            pltpu.make_async_copy(
                src.at[pl.ds(n * rows, rows)], both_ref.at[pl.ds(n * rows, rows), pl.ds(k * h, h)], sems.at[k, n]
            )
            for n in range(parts)
        ]
        for k, src in enumerate(columns)
    ]
    last = pltpu.make_async_copy(down_hbm, down_ref, last_sem)
    for copy in copies[0] + copies[1] + [last]:
        copy.start()
    for k, turned_ref in enumerate((gate_ref, up_ref)):
        for n, copy in enumerate(copies[k]):
            copy.wait()
            here = slice(n * rows, (n + 1) * rows)
            turned_ref[:, here] = both_ref[here, k * h : (k + 1) * h].T
    last.wait()


def turn(down_ref, after, turned_ref):
    d = turned_ref.shape[0]
    step = d // 8
    for n in range(0, d, step):
        turned_ref[n : n + step] = down_ref[:, n : n + step].T


def collect(turns, *refs):
    *blocks, after, out_ref, gain_ref = refs
    r = blocks[0].shape[0]
    first, turned = on_first_core(), on_chip_with(turns)
    came = [ref[:, : out_ref.shape[1]] for ref in blocks[::-1]]
    nearer = came[-1:] + came[:-1]
    farther = crossed(came, turned) if turns else came
    for n, (a, b) in enumerate(zip(nearer, farther)):
        out_ref[n * r : (n + 1) * r] = jnp.where(first, a, b)
    width = out_ref.shape[1]
    piece = blocks[0].shape[1] - width
    for n in range(r):
        gain_ref[:, n * piece : (n + 1) * piece] = blocks[0][n : n + 1, width:].astype(jnp.float32)


def arrange(near_ref, far_ref, gain_ref, normed_ref, grad_ref, own_ref, rows_ref):
    d = normed_ref.shape[1]
    half, r = near_ref.shape[0], own_ref.shape[0]
    first = on_first_core()
    near, far = near_ref[...], far_ref[...]
    for at, rows in ((0, jnp.where(first, near, far)), (half, jnp.where(first, far, near))):
        rows_ref[at : at + half] = rows[:, :d].astype(jnp.float32)
        grad_ref[at : at + half] = rows[:, d:]
        if at == 0:
            own_ref[:, : 2 * d] = jnp.where(first, rows[:r], rows[r : 2 * r])
    wide = rows_ref[...]
    recip = lax.rsqrt(jnp.mean(wide * wide, axis=-1, keepdims=True) + EPS)
    normed_ref[...] = (wide * recip * gain_ref[...]).astype(jnp.bfloat16)
    piece = d // r
    for n in range(r):
        own_ref[n : n + 1, 2 * d :] = gain_ref[:, n * piece : (n + 1) * piece].astype(jnp.bfloat16)


def expert(rows, normed_ref, grad_ref, both_ref, gate_ref, up_ref, down_ref, mine_ref, other_ref):
    h = down_ref.shape[1]
    both = nn(normed_ref[...], both_ref[...])
    gate, up = both[:, :h], both[:, h:]
    d_hidden = nn(grad_ref[...], down_ref[...])
    p = jax.nn.sigmoid(gate)
    d_gate = d_hidden * up * p * (1.0 + gate * (1.0 - p))
    d_up = d_hidden * gate * p
    d_both = jnp.concatenate([d_gate, d_up], axis=1).astype(jnp.bfloat16)
    total = nn(d_both[:, :h], gate_ref[...]) + nn(d_both[:, h:], up_ref[...])
    first = on_first_core()
    for n in range(mine_ref.shape[0] // rows):
        even = total[2 * n * rows : (2 * n + 1) * rows]
        odd = total[(2 * n + 1) * rows : (2 * n + 2) * rows]
        mine_ref[n * rows : (n + 1) * rows] = jnp.where(first, even, odd)
        other_ref[n * rows : (n + 1) * rows] = jnp.where(first, odd, even)


def add_cores(turns, mine_ref, got_ref, *out_refs):
    total = (mine_ref[...] + got_ref[...]).astype(jnp.bfloat16)
    r = out_refs[0].shape[0]
    parts = [total[k * r : (k + 1) * r] for k in range(len(out_refs))]
    first = on_first_core()
    odd = crossed(parts, jnp.logical_not(on_chip_with(turns))) if turns else parts
    for ref, a, b in zip(out_refs, parts[::-1], odd):
        ref[...] = jnp.where(first, a, b)


def add_chips(stays, local_ref, *refs):
    *parts, keep_ref, send_ref = refs
    first = on_first_core()
    stayed = jnp.logical_and(first, stays(lax.axis_index("section")))
    total = jnp.where(stayed, local_ref[...], parts[-1][...]).astype(jnp.float32)
    for ref in parts[:-1]:
        total = total + ref[...].astype(jnp.float32)
    r = keep_ref.shape[0]
    keep_ref[...] = jnp.where(first, total[:r], total[r:])
    send_ref[...] = jnp.where(first, total[r:], total[:r])


def settle(stays, stayed_ref, moved_ref, keep_ref, unit_ref, gain_ref, kept_ref, base_ref, recip_ref):
    r, d = keep_ref.shape
    here = stays(lax.axis_index("section"))
    own = jnp.where(here, stayed_ref[...].astype(jnp.float32), moved_ref[...].astype(jnp.float32))
    piece = d // r
    for n in range(r):
        gain_ref[:, n * piece : (n + 1) * piece] = own[n : n + 1, 2 * d :]
    wide = own[:, :d]
    recip = lax.rsqrt(jnp.mean(wide * wide, axis=-1, keepdims=True) + EPS)
    unit_ref[...] = wide * recip
    kept_ref[...] = gain_ref[...] * keep_ref[...]
    base_ref[...] = own[:, d : 2 * d]
    recip_ref[...] = jnp.broadcast_to(recip, recip_ref.shape)


def finish(unit_ref, gain_ref, kept_ref, base_ref, recip_ref, got_ref, out_ref):
    unit, recip = unit_ref[...], recip_ref[:, :1]
    scaled = kept_ref[...] + gain_ref[...] * got_ref[...]
    mean = jnp.mean(scaled * unit, axis=-1, keepdims=True)
    out_ref[0] = (base_ref[...] + recip * (scaled - unit * mean)).astype(out_ref.dtype)


def on_device(sections, members, saved_in, grad_in, slot_table, gain, w_gate, w_up, w_down):
    chips = members // CORES
    r, d = grad_in.shape[1:]
    hidden = w_down.shape[0]
    f32, bf16 = jnp.float32, jnp.bfloat16
    half = chips // CORES
    power = chips & (chips - 1) == 0
    out_turns, home_turns = (half, 1) if power else (0, 0)

    def swapped(n, t, bit, chip):
        return t ^ 1 if bit and chip & bit and t | 1 < n else t

    def route(goal):
        pairs = []
        for s in range(sections):
            for i in range(members):
                to, chip, *core = goal(s, *divmod(i, CORES))
                core = core[0] if core else i % CORES
                pairs.append((s * members + i, to % sections * members + chip % chips * CORES + core))
        return pairs

    even = sections % 2 == 0

    def beside(s):
        return s ^ 1 if even else s - 1

    def before(s):
        return s - 2 * (s % 2) if even else s

    def stays(section):
        return lax.rem(section, 2) == 0 if even else section >= 0

    def ahead(x, t):
        def goal(s, chip, core):
            k = half + swapped(half, t, out_turns, chip) if core else (t + 1) % half
            return beside(s), chip ^ k if power else chip + k

        return lax.ppermute(x, ("section", "seqtp"), route(goal))

    def home(x, t):
        def goal(s, chip, core):
            k = 2 * swapped(half, t, home_turns, chip) + 1 if core else 2 * (half - 1 - t)
            to = before(s) if k else s - 2 if even else s - 1
            return to, chip ^ k if power else chip - k

        return lax.ppermute(x, ("section", "seqtp"), route(goal))

    def back(x):
        return lax.ppermute(x, ("section", "seqtp"), route(lambda s, chip, core: (s, chip, core ^ 1) if before(s) == s else (before(s), chip)))

    def to_core(x):
        return lax.ppermute(x, "seqtp", [(i, i ^ 1) for i in range(members)])

    scalar = pl.BlockSpec(memory_space=pltpu.SMEM)
    mine, gain_row = pl.pallas_call(
        prepare,
        out_shape=[VMEM((r, 2 * d), bf16), VMEM(gain.shape, bf16)],
        in_specs=[scalar] + anywhere(3),
        out_specs=whole(2),
        scratch_shapes=[pltpu.SemaphoreType.DMA((3,))],
        compiler_params=params(4),
        name="prepare",
    )(slot_table, *far_off(saved_in, grad_in, gain))
    chip_rows = pl.pallas_call(
        join,
        out_shape=VMEM((CORES * r, 2 * d + d // (CORES * r)), bf16),
        in_specs=[scalar] + whole(4),
        out_specs=pl.BlockSpec(memory_space=VMEM),
        compiler_params=params(4),
        name="join",
    )(slot_table, *near_core(mine, to_core(saved_in), to_core(grad_in), gain_row))
    both, gate_turned, up_turned, down = pl.pallas_call(
        fetch,
        out_shape=[VMEM((d, 2 * hidden), bf16)] + [VMEM((hidden, d), bf16)] * 3,
        in_specs=anywhere(3),
        out_specs=whole(4),
        scratch_shapes=[pltpu.SemaphoreType.DMA((2, 4)), pltpu.SemaphoreType.DMA],
        compiler_params=params(4),
        cost_estimate=cost(12 * d * hidden),
        name="fetch",
    )(*far_off(w_gate, w_up, w_down))
    blocks = [ahead(chip_rows, t) for t in range(half)]
    rows = chips * r
    block, gain_wide = pl.pallas_call(
        functools.partial(collect, out_turns),
        out_shape=[VMEM((rows, 2 * d), bf16), VMEM((1, d), f32)],
        in_specs=whole(len(blocks)) + anywhere(1),
        out_specs=whole(2),
        compiler_params=params(4),
        name="collect",
    )(*near_core(*blocks[::-1], both))
    far = to_core(block)
    down_turned = pl.pallas_call(
        turn,
        out_shape=VMEM((d, hidden), bf16),
        in_specs=whole(1) + anywhere(1),
        out_specs=pl.BlockSpec(memory_space=VMEM),
        compiler_params=params(4),
        cost_estimate=cost(4 * d * hidden),
        name="turn",
    )(*near_core(down, block))
    normed, grad, own = pl.pallas_call(
        arrange,
        out_shape=[VMEM((2 * rows, d), bf16)] * 2 + [VMEM((r, 2 * d + d // r), bf16)],
        in_specs=whole(3),
        out_specs=whole(3),
        scratch_shapes=[VMEM((2 * rows, d), f32)],
        compiler_params=params(16),
        name="arrange",
    )(*near_core(block, far, gain_wide))
    mine, other = pl.pallas_call(
        functools.partial(expert, CORES * r),
        out_shape=[VMEM((rows, d), f32)] * 2,
        in_specs=whole(6),
        out_specs=whole(2),
        compiler_params=params(16),
        name="expert",
    )(*near_core(normed, grad, both, gate_turned, up_turned, down_turned))
    sums = pl.pallas_call(
        functools.partial(add_cores, home_turns),
        out_shape=[VMEM((CORES * r, d), bf16)] * half,
        in_specs=whole(2),
        out_specs=whole(half),
        compiler_params=params(4),
        name="add_cores",
    )(*near_core(mine, to_core(other)))
    landed = [home(x, t) for t, x in enumerate(sums)]
    moved = back(own)
    keep, send = pl.pallas_call(
        functools.partial(add_chips, stays),
        out_shape=[VMEM((r, d), f32)] * 2,
        in_specs=whole(1 + half),
        out_specs=whole(2),
        compiler_params=params(4),
        name="add_chips",
    )(*near_core(sums[-1], *landed))
    settled = pl.pallas_call(
        functools.partial(settle, stays),
        out_shape=[VMEM(dims, f32) for dims in ((r, d), (1, d), (r, d), (r, d), (r, 128))],
        in_specs=whole(3),
        out_specs=whole(5),
        compiler_params=params(4),
        name="settle",
    )(*near_core(own, moved, keep))
    return pl.pallas_call(
        finish,
        out_shape=jax.ShapeDtypeStruct((1, r, d), bf16),
        in_specs=whole(6),
        out_specs=pl.BlockSpec(memory_space=VMEM),
        compiler_params=params(4),
        name="finish",
    )(*near_core(*settled, to_core(send)))


def solution(mesh):
    return jax.shard_map(
        functools.partial(on_device, mesh.shape["section"], mesh.shape["seqtp"]),
        mesh=mesh,
        in_specs=(
            P("section", None, "seqtp", None),
            P("section", "seqtp", None),
            P("section"),
            P("section", None),
            P(None, "seqtp"),
            P(None, "seqtp"),
            P("seqtp", None),
        ),
        out_specs=P("section", "seqtp", None),
        check_vma=False,
    )
```

```python
import functools

import jax
import jax.numpy as jnp
from jax import lax
from jax.experimental import pallas as pl
from jax.experimental.pallas import tpu as pltpu
from jax.sharding import PartitionSpec as P

EPS = 1e-05
CORES = 2
VMEM = pltpu.VMEM


def whole(n):
    return [pl.BlockSpec(memory_space=VMEM)] * n


def anywhere(n):
    return [pl.BlockSpec(memory_space=pl.ANY)] * n


def near_core(*arrays):
    return [pltpu.with_memory_space_constraint(x, VMEM) for x in arrays]


def far_off(*arrays):
    return [pltpu.with_memory_space_constraint(x, pltpu.HBM) for x in arrays]


def params(mib):
    return pltpu.CompilerParams(vmem_limit_bytes=mib * 2**20)


def cost(bytes_accessed):
    return pl.CostEstimate(flops=0, bytes_accessed=bytes_accessed, transcendentals=0)


def on_chip_with(bit):
    return lax.rem(lax.div(lax.axis_index("seqtp"), CORES * max(bit, 1)), 2) == 1


def crossed(blocks, swap):
    out = list(blocks)
    for n in range(0, len(blocks) - 1, 2):
        a, b = blocks[n : n + 2]
        out[n], out[n + 1] = jnp.where(swap, a, b), jnp.where(swap, b, a)
    return out


def on_first_core():
    return lax.rem(lax.axis_index("seqtp"), CORES) == 0


def nn(left, weight):
    return jnp.dot(left, weight, preferred_element_type=jnp.float32)


def prepare(slot_ref, saved_hbm, grad_hbm, gain_hbm, mine_ref, gain_ref, sems):
    d = grad_hbm.shape[-1]
    copies = [
        pltpu.make_async_copy(src, dst, sems.at[n])
        for n, (src, dst) in enumerate(
            (
                (saved_hbm.at[0, slot_ref[0]], mine_ref.at[:, pl.ds(0, d)]),
                (grad_hbm.at[0], mine_ref.at[:, pl.ds(d, d)]),
                (gain_hbm, gain_ref),
            )
        )
    ]
    for copy in copies:
        copy.start()
    for copy in copies:
        copy.wait()


def join(slot_ref, mine_ref, saved_ref, grad_ref, gain_ref, rows_ref):
    r, d = grad_ref.shape[1:]
    first = on_first_core()
    for at, other in enumerate((saved_ref[0, slot_ref[0]], grad_ref[0])):
        part = slice(at * d, (at + 1) * d)
        mine = mine_ref[:, part]
        rows_ref[:r, part] = jnp.where(first, mine, other)
        rows_ref[r:, part] = jnp.where(first, other, mine)
    piece = rows_ref.shape[1] - 2 * d
    for n in range(rows_ref.shape[0]):
        rows_ref[n : n + 1, 2 * d :] = gain_ref[:, n * piece : (n + 1) * piece]


def fetch(gate_hbm, up_hbm, down_hbm, both_ref, gate_ref, up_ref, down_ref, sems, last_sem):
    d, h = gate_hbm.shape
    parts = sems.shape[1]
    rows = d // parts
    columns = (gate_hbm, up_hbm)
    copies = [
        [
            pltpu.make_async_copy(
                src.at[pl.ds(n * rows, rows)], both_ref.at[pl.ds(n * rows, rows), pl.ds(k * h, h)], sems.at[k, n]
            )
            for n in range(parts)
        ]
        for k, src in enumerate(columns)
    ]
    last = pltpu.make_async_copy(down_hbm, down_ref, last_sem)
    for copy in copies[0] + copies[1] + [last]:
        copy.start()
    for k, turned_ref in enumerate((gate_ref, up_ref)):
        for n, copy in enumerate(copies[k]):
            copy.wait()
            here = slice(n * rows, (n + 1) * rows)
            turned_ref[:, here] = both_ref[here, k * h : (k + 1) * h].T
    last.wait()


def turn(down_ref, after, turned_ref):
    d = turned_ref.shape[0]
    step = d // 8
    for n in range(0, d, step):
        turned_ref[n : n + step] = down_ref[:, n : n + step].T


def collect(turns, *refs):
    *blocks, after, out_ref, gain_ref = refs
    r = blocks[0].shape[0]
    first, turned = on_first_core(), on_chip_with(turns)
    came = [ref[:, : out_ref.shape[1]] for ref in blocks[::-1]]
    nearer = came[-1:] + came[:-1]
    farther = crossed(came, turned) if turns else came
    for n, (a, b) in enumerate(zip(nearer, farther)):
        out_ref[n * r : (n + 1) * r] = jnp.where(first, a, b)
    width = out_ref.shape[1]
    piece = blocks[0].shape[1] - width
    for n in range(r):
        gain_ref[:, n * piece : (n + 1) * piece] = blocks[0][n : n + 1, width:].astype(jnp.float32)


def arrange(near_ref, far_ref, gain_ref, normed_ref, grad_ref, own_ref, rows_ref):
    d = normed_ref.shape[1]
    half, r = near_ref.shape[0], own_ref.shape[0]
    first = on_first_core()
    near, far = near_ref[...], far_ref[...]
    for at, rows in ((0, jnp.where(first, near, far)), (half, jnp.where(first, far, near))):
        rows_ref[at : at + half] = rows[:, :d].astype(jnp.float32)
        grad_ref[at : at + half] = rows[:, d:]
        if at == 0:
            own_ref[:, : 2 * d] = jnp.where(first, rows[:r], rows[r : 2 * r])
    wide = rows_ref[...]
    recip = lax.rsqrt(jnp.mean(wide * wide, axis=-1, keepdims=True) + EPS)
    normed_ref[...] = (wide * recip * gain_ref[...]).astype(jnp.bfloat16)
    piece = d // r
    for n in range(r):
        own_ref[n : n + 1, 2 * d :] = gain_ref[:, n * piece : (n + 1) * piece].astype(jnp.bfloat16)


def expert(rows, normed_ref, grad_ref, both_ref, gate_ref, up_ref, down_ref, mine_ref, other_ref):
    h = down_ref.shape[1]
    both = nn(normed_ref[...], both_ref[...])
    gate, up = both[:, :h], both[:, h:]
    d_hidden = nn(grad_ref[...], down_ref[...])
    p = jax.nn.sigmoid(gate)
    d_gate = d_hidden * up * p * (1.0 + gate * (1.0 - p))
    d_up = d_hidden * gate * p
    d_both = jnp.concatenate([d_gate, d_up], axis=1).astype(jnp.bfloat16)
    total = nn(d_both[:, :h], gate_ref[...]) + nn(d_both[:, h:], up_ref[...])
    first = on_first_core()
    for n in range(mine_ref.shape[0] // rows):
        even = total[2 * n * rows : (2 * n + 1) * rows]
        odd = total[(2 * n + 1) * rows : (2 * n + 2) * rows]
        mine_ref[n * rows : (n + 1) * rows] = jnp.where(first, even, odd)
        other_ref[n * rows : (n + 1) * rows] = jnp.where(first, odd, even)


def add_cores(turns, mine_ref, got_ref, *out_refs):
    total = (mine_ref[...] + got_ref[...]).astype(jnp.bfloat16)
    r = out_refs[0].shape[0]
    parts = [total[k * r : (k + 1) * r] for k in range(len(out_refs))]
    first = on_first_core()
    odd = crossed(parts, jnp.logical_not(on_chip_with(turns))) if turns else parts
    for ref, a, b in zip(out_refs, parts[::-1], odd):
        ref[...] = jnp.where(first, a, b)


def add_chips(stays, local_ref, *refs):
    *parts, keep_ref, send_ref = refs
    first = on_first_core()
    stayed = jnp.logical_and(first, stays(lax.axis_index("section")))
    total = jnp.where(stayed, local_ref[...], parts[-1][...]).astype(jnp.float32)
    for ref in parts[:-1]:
        total = total + ref[...].astype(jnp.float32)
    r = keep_ref.shape[0]
    keep_ref[...] = jnp.where(first, total[:r], total[r:])
    send_ref[...] = jnp.where(first, total[r:], total[:r])


def settle(stays, stayed_ref, moved_ref, keep_ref, unit_ref, gain_ref, kept_ref, base_ref, recip_ref):
    r, d = keep_ref.shape
    here = stays(lax.axis_index("section"))
    own = jnp.where(here, stayed_ref[...].astype(jnp.float32), moved_ref[...].astype(jnp.float32))
    piece = d // r
    for n in range(r):
        gain_ref[:, n * piece : (n + 1) * piece] = own[n : n + 1, 2 * d :]
    wide = own[:, :d]
    recip = lax.rsqrt(jnp.mean(wide * wide, axis=-1, keepdims=True) + EPS)
    unit_ref[...] = wide * recip
    kept_ref[...] = gain_ref[...] * keep_ref[...]
    base_ref[...] = own[:, d : 2 * d]
    recip_ref[...] = jnp.broadcast_to(recip, recip_ref.shape)


def finish(unit_ref, gain_ref, kept_ref, base_ref, recip_ref, got_ref, out_ref):
    unit, recip = unit_ref[...], recip_ref[:, :1]
    scaled = kept_ref[...] + gain_ref[...] * got_ref[...]
    mean = jnp.mean(scaled * unit, axis=-1, keepdims=True)
    out_ref[0] = (base_ref[...] + recip * (scaled - unit * mean)).astype(out_ref.dtype)


def on_device(sections, members, saved_in, grad_in, slot_table, gain, w_gate, w_up, w_down):
    chips = members // CORES
    r, d = grad_in.shape[1:]
    hidden = w_down.shape[0]
    f32, bf16 = jnp.float32, jnp.bfloat16
    half = chips // CORES
    power = chips & (chips - 1) == 0
    out_turns, home_turns = (half, 1) if power else (0, 0)

    def swapped(n, t, bit, chip):
        return t ^ 1 if bit and chip & bit and t | 1 < n else t

    def route(goal):
        pairs = []
        for s in range(sections):
            for i in range(members):
                to, chip, *core = goal(s, *divmod(i, CORES))
                core = core[0] if core else i % CORES
                pairs.append((s * members + i, to % sections * members + chip % chips * CORES + core))
        return pairs

    even = sections % 2 == 0

    def beside(s):
        return s ^ 1 if even else s - 1

    def before(s):
        return s - 2 * (s % 2) if even else s

    def stays(section):
        return lax.rem(section, 2) == 0 if even else section >= 0

    def ahead(x, t):
        def goal(s, chip, core):
            k = half + swapped(half, t, out_turns, chip) if core else (t + 1) % half
            return beside(s), chip ^ k if power else chip + k

        return lax.ppermute(x, ("section", "seqtp"), route(goal))

    def home(x, t):
        def goal(s, chip, core):
            k = 2 * swapped(half, t, home_turns, chip) + 1 if core else 2 * (half - 1 - t)
            to = before(s) if k else s - 2 if even else s - 1
            return to, chip ^ k if power else chip - k

        return lax.ppermute(x, ("section", "seqtp"), route(goal))

    def back(x):
        return lax.ppermute(x, ("section", "seqtp"), route(lambda s, chip, core: (s, chip, core ^ 1) if before(s) == s else (before(s), chip)))

    def to_core(x):
        return lax.ppermute(x, "seqtp", [(i, i ^ 1) for i in range(members)])

    scalar = pl.BlockSpec(memory_space=pltpu.SMEM)
    mine, gain_row = pl.pallas_call(
        prepare,
        out_shape=[VMEM((r, 2 * d), bf16), VMEM(gain.shape, bf16)],
        in_specs=[scalar] + anywhere(3),
        out_specs=whole(2),
        scratch_shapes=[pltpu.SemaphoreType.DMA((3,))],
        compiler_params=params(4),
        name="prepare",
    )(slot_table, *far_off(saved_in, grad_in, gain))
    chip_rows = pl.pallas_call(
        join,
        out_shape=VMEM((CORES * r, 2 * d + d // (CORES * r)), bf16),
        in_specs=[scalar] + whole(4),
        out_specs=pl.BlockSpec(memory_space=VMEM),
        compiler_params=params(4),
        name="join",
    )(slot_table, *near_core(mine, to_core(saved_in), to_core(grad_in), gain_row))
    both, gate_turned, up_turned, down = pl.pallas_call(
        fetch,
        out_shape=[VMEM((d, 2 * hidden), bf16)] + [VMEM((hidden, d), bf16)] * 3,
        in_specs=anywhere(3),
        out_specs=whole(4),
        scratch_shapes=[pltpu.SemaphoreType.DMA((2, 2)), pltpu.SemaphoreType.DMA],
        compiler_params=params(4),
        cost_estimate=cost(12 * d * hidden),
        name="fetch",
    )(*far_off(w_gate, w_up, w_down))
    blocks = [ahead(chip_rows, t) for t in range(half)]
    rows = chips * r
    block, gain_wide = pl.pallas_call(
        functools.partial(collect, out_turns),
        out_shape=[VMEM((rows, 2 * d), bf16), VMEM((1, d), f32)],
        in_specs=whole(len(blocks)) + anywhere(1),
        out_specs=whole(2),
        compiler_params=params(4),
        name="collect",
    )(*near_core(*blocks[::-1], both))
    far = to_core(block)
    down_turned = pl.pallas_call(
        turn,
        out_shape=VMEM((d, hidden), bf16),
        in_specs=whole(1) + anywhere(1),
        out_specs=pl.BlockSpec(memory_space=VMEM),
        compiler_params=params(4),
        cost_estimate=cost(4 * d * hidden),
        name="turn",
    )(*near_core(down, block))
    normed, grad, own = pl.pallas_call(
        arrange,
        out_shape=[VMEM((2 * rows, d), bf16)] * 2 + [VMEM((r, 2 * d + d // r), bf16)],
        in_specs=whole(3),
        out_specs=whole(3),
        scratch_shapes=[VMEM((2 * rows, d), f32)],
        compiler_params=params(16),
        name="arrange",
    )(*near_core(block, far, gain_wide))
    mine, other = pl.pallas_call(
        functools.partial(expert, CORES * r),
        out_shape=[VMEM((rows, d), f32)] * 2,
        in_specs=whole(6),
        out_specs=whole(2),
        compiler_params=params(16),
        name="expert",
    )(*near_core(normed, grad, both, gate_turned, up_turned, down_turned))
    sums = pl.pallas_call(
        functools.partial(add_cores, home_turns),
        out_shape=[VMEM((CORES * r, d), bf16)] * half,
        in_specs=whole(2),
        out_specs=whole(half),
        compiler_params=params(4),
        name="add_cores",
    )(*near_core(mine, to_core(other)))
    landed = [home(x, t) for t, x in enumerate(sums)]
    moved = back(own)
    keep, send = pl.pallas_call(
        functools.partial(add_chips, stays),
        out_shape=[VMEM((r, d), f32)] * 2,
        in_specs=whole(1 + half),
        out_specs=whole(2),
        compiler_params=params(4),
        name="add_chips",
    )(*near_core(sums[-1], *landed))
    settled = pl.pallas_call(
        functools.partial(settle, stays),
        out_shape=[VMEM(dims, f32) for dims in ((r, d), (1, d), (r, d), (r, d), (r, 128))],
        in_specs=whole(3),
        out_specs=whole(5),
        compiler_params=params(4),
        name="settle",
    )(*near_core(own, moved, keep))
    return pl.pallas_call(
        finish,
        out_shape=jax.ShapeDtypeStruct((1, r, d), bf16),
        in_specs=whole(6),
        out_specs=pl.BlockSpec(memory_space=VMEM),
        compiler_params=params(4),
        name="finish",
    )(*near_core(*settled, to_core(send)))


def solution(mesh):
    return jax.shard_map(
        functools.partial(on_device, mesh.shape["section"], mesh.shape["seqtp"]),
        mesh=mesh,
        in_specs=(
            P("section", None, "seqtp", None),
            P("section", "seqtp", None),
            P("section"),
            P("section", None),
            P(None, "seqtp"),
            P(None, "seqtp"),
            P("seqtp", None),
        ),
        out_specs=P("section", "seqtp", None),
        check_vma=False,
    )
```
